128 devices in a mesh: ba: 8 (over z, core), bb: 16 (over y, x).
Axes of the slice: x: 4, y: 4, z: 4, core: 2. Of those that a mesh axis runs over, the one named last changes fastest.
Arguments:
- tensor: bfloat16 [2, 64, 5, 384, 384], P(None, 'ba', None, 'bb'), may hold values from -6 to 6
- occupied: bfloat16 [64, 3, 384, 384], P('ba', None, 'bb'), may hold values from -0.1875 to 0.1875
- virtual: bfloat16 [64, 3, 384, 384], P('ba', None, 'bb'), may hold values from -0.1875 to 0.1875
- tensor_mask: int32 [64, 5], replicated, may hold values 0 or 1
- occupied_mask: int32 [64, 3], replicated, may hold values 0 or 1
- virtual_mask: int32 [64, 3], replicated, may hold values 0 or 1
Outputs:
- product_slab: bfloat16 [2, 64, 5, 384, 384], P(None, 'ba', None, 'bb')
- coupling: float32 [2, 2], replicated
The draws below stay inside these ranges and needn't reach their ends.
All inputs are finite; a program needn't handle non-finite values.
Results may differ from the reference program's by a relative error of at most 0.0067.
Values may be sent and summed in bfloat16 or wider, within the bound.
A program may use at most 128 MiB of HBM per device.

```python
import math
import jax
import jax.numpy as jnp
from jax import lax

BASIS = 24576
BLK = 384
HB = 5
HG = 3
PS = 2
NB = 64
HX = 7


def touch_ends(drawn, key, smallest, high):
    shape = drawn.shape
    index_at = [jax.random.randint(jax.random.fold_in(key, axis), (), 0, shape[axis]) for axis in range(len(shape))]
    drawn = drawn.at[tuple(index_at)].set(smallest)
    longest = shape.index(max(shape))
    index_at[longest] = (index_at[longest] + 1) % shape[longest]
    return drawn.at[tuple(index_at)].set(high)


def block_scale(own_key, shape, split, smallest, largest):
    gain, own = 1.0, jax.random.fold_in(own_key, 6)
    for position, parts in split:
        steps = jnp.exp(jax.random.uniform(jax.random.fold_in(own, position), (parts,), jnp.float32, smallest / len(split), largest / len(split)))
        gain = gain * jnp.repeat(steps, shape[position] // parts).reshape([-1 if axis == position else 1 for axis in range(len(shape))])
    return gain


def gaussian(key, extent, deviation, limit, pieces=(), dtype=jnp.bfloat16):
    values = deviation * jax.random.normal(key, extent, jnp.float32)
    if pieces:
        values = values * block_scale(key, extent, pieces, -0.22, 0.18)
    return jnp.clip(values, -limit, limit).astype(dtype)


def setup_inputs(seed: int = 0) -> dict:
    seeds = jax.random.split(jax.random.key(seed), 7)
    return {
        "tensor": gaussian(seeds[0], (PS, NB, HB, BLK, BLK), 1.0, 6.0, ((1, 8), (3, 16))),
        "occupied": gaussian(seeds[1], (NB, HG, BLK, BLK), (HG * BLK) ** -0.5, 0.1875, ((0, 8), (2, 16))),
        "virtual": gaussian(seeds[2], (NB, HG, BLK, BLK), (HG * BLK) ** -0.5, 0.1875, ((0, 8), (2, 16))),
        "tensor_mask": touch_ends((jax.random.randint(seeds[3], (NB, HB), 0, 4) < 3).astype(jnp.int32), jax.random.fold_in(seeds[3], 1), 0, 1),
        "occupied_mask": touch_ends((jax.random.randint(seeds[4], (NB, HG), 0, 4) < 3).astype(jnp.int32), jax.random.fold_in(seeds[4], 1), 0, 1),
        "virtual_mask": touch_ends((jax.random.randint(seeds[5], (NB, HG), 0, 4) < 3).astype(jnp.int32), jax.random.fold_in(seeds[5], 1), 0, 1),
    }


def reference(tensor, occupied, virtual, tensor_mask, occupied_mask, virtual_mask):
    masked = tensor * tensor_mask.astype(jnp.bfloat16)[None, :, :, None, None]
    occ_full = (occupied * occupied_mask.astype(jnp.bfloat16)[:, :, None, None]).astype(jnp.float32)
    vir_full = (virtual * virtual_mask.astype(jnp.bfloat16)[:, :, None, None]).astype(jnp.float32)
    radius_b = HB // 2
    radius_g = HG // 2
    pattern = tensor_mask.astype(jnp.float32)[:, :, None, None]

    def one_function(slab_piece):
        piece = slab_piece.astype(jnp.float32)
        partial_value = [jnp.zeros((NB, BLK, BLK), jnp.float32) for offset in range(HX)]
        for shift_b in range(HB):
            rolled = jnp.roll(occ_full, -(shift_b - radius_b), axis=0)
            for shift_g in range(HG):
                partial_value[shift_b + shift_g] = partial_value[shift_b + shift_g] + jnp.einsum('irc,icd->ird', piece[:, shift_b], rolled[:, shift_g])
        inter = jnp.stack(partial_value, axis=1).astype(jnp.bfloat16)
        inter = lax.optimization_barrier(inter).astype(jnp.float32)
        result = []
        for target in range(HB):
            summed = jnp.zeros((NB, BLK, BLK), jnp.float32)
            for shift_g in range(HG):
                offset = target + 2 * radius_g - shift_g
                rows_x = jnp.roll(inter, -(shift_g - radius_g), axis=0)[:, offset]
                summed = summed + jnp.einsum('sab,sbc->sac', vir_full[:, shift_g], rows_x)
            result.append(summed)
        return (jnp.stack(result, axis=1) * pattern).astype(jnp.bfloat16)
    product_slab = lax.map(one_function, masked)
    flat_y = product_slab.reshape(PS, -1)
    flat_b = masked.reshape(PS, -1)
    coupling = jnp.dot(flat_y, flat_b.T, preferred_element_type=jnp.float32) / math.sqrt(BASIS * HB * BLK)
    return (product_slab, coupling)
```

```python
import math

import jax
import jax.numpy as jnp
from jax import lax
from jax.experimental import pallas as pl
from jax.experimental.pallas import tpu as pltpu
from jax.sharding import PartitionSpec as P

BASIS = 24576
BLK = 384
HB = 5
MESH = pl.DeviceIdType.MESH
VMEM_LIMIT = 56 * 1024 * 1024

T_ROWS = 128
V_ROWS = 80
O_ROWS = 144
E_ROWS = 32
O_SPAN = ((16, 128), (0, 144), (0, 128))

ORDER = (
    (0, 0), (2, 2), (1, 0), (0, 1), (3, 0), (0, 3), (1, 1), (3, 3),
    (1, 3), (3, 1), (2, 0), (0, 2), (2, 1), (1, 2), (2, 3), (3, 2),
)


def pick(table, index):
    value = 0
    for position, entry in enumerate(table):
        if entry:
            value = value + jnp.where(index == position, entry, 0)
    return value


def chip_of(p, j):
    x = jnp.where(j < 4, j, 7 - j)
    y = jnp.where(j < 4, p, 3 - p)
    return y * 4 + x


def work_of(chip):
    x, y = chip % 4, chip // 4
    upper = y >= 2
    j = jnp.where(upper, 7 - x, x)
    p = jnp.where(upper, 3 - y, y)
    return p, j


def target_chip(step, chip, core):
    dx, dy = pick([d[0] for d in ORDER], step), pick([d[1] for d in ORDER], step)
    ex = jnp.where(core == 0, dx, dy)
    ey = jnp.where(core == 0, dy, dx)
    return ((chip // 4 + ey) % 4) * 4 + (chip % 4 + ex) % 4


def place():
    a, chip = lax.axis_index("ba"), lax.axis_index("bb")
    return a, chip, a // 2, a % 2


def greet(bar, a, b):
    pl.semaphore_signal(bar, inc=1, device_id=(a, b), device_id_type=MESH)


def plane_barrier(bar, a, z, chip):
    def hello(k, carry):
        other_a, other_chip = 2 * z + k // 16, k % 16

        @pl.when(jnp.logical_not((other_a == a) & (other_chip == chip)))
        def _():
            greet(bar, other_a, other_chip)

        return carry

    lax.fori_loop(0, 32, hello, 0)


def drain(count, ref, sem):
    def one(k, carry):
        pltpu.make_async_copy(ref, ref, sem).wait()
        return carry

    lax.fori_loop(0, count, one, 0)


def send(cond, is_self, src, dst, send_sem, recv_sem, device):
    @pl.when(cond & is_self)
    def _():
        pltpu.make_async_copy(src, dst, recv_sem).start()

    @pl.when(cond & jnp.logical_not(is_self))
    def _():
        pltpu.make_async_remote_copy(
            src_ref=src, dst_ref=dst, send_sem=send_sem, recv_sem=recv_sem,
            device_id=device, device_id_type=MESH,
        ).start()

    return jnp.where(cond & jnp.logical_not(is_self), 1, 0)


def gather_kernel(
    t_ref, v_ref, o_ref, tr_ref, vr_ref, or_ref, er_ref,
    t_send, t_recv, v_send, v_recv, o_send, o_recv, e_send, e_recv,
    f_send, f_recv, h_send, h_recv,
):
    a, chip, z, core = place()
    p_me, j_me = work_of(chip)
    bar = pltpu.get_barrier_semaphore()
    plane_barrier(bar, a, z, chip)

    @pl.when(j_me < 2)
    def _():
        def hello(k, carry):
            greet(bar, (2 * z + 7) % 8, k)
            return carry

        lax.fori_loop(0, 16, hello, 0)

    @pl.when(j_me >= 6)
    def _():
        def hello(k, carry):
            greet(bar, (2 * z + 2) % 8, k)
            return carry

        lax.fori_loop(0, 16, hello, 0)

    s_here = 2 * j_me + core
    up_in = s_here < 15
    down_in = s_here > 0
    up_j = jnp.where(core == 0, j_me, (j_me + 1) % 8)
    up_z = jnp.where(up_in, z, (z + 1) % 4)
    down_j = jnp.where(core == 1, j_me, (j_me + 7) % 8)
    down_z = jnp.where(down_in, z, (z + 3) % 4)
    up = (2 * up_z + 1 - core, chip_of(p_me, up_j))
    down = (2 * down_z + 1 - core, chip_of(p_me, down_j))

    pl.semaphore_wait(bar, 39)

    def send_t(step, count):
        chip_to = target_chip(step, chip, core)
        p, j = work_of(chip_to)
        mine = j // 4 == core
        for half in range(2):
            il = jnp.where(mine, 2 * (j - 4 * core) + half, 0)
            count = count + send(
                mine, (chip_to == chip) & (core == half),
                t_ref.at[p, il], tr_ref.at[1, chip], t_send, t_recv,
                (2 * z + half, chip_to),
            )
        return count

    t_count = lax.fori_loop(0, 16, send_t, 0)

    o_core = chip // 8

    def send_rest(step, counts):
        v_count, o0, o1, o2, e_count = counts
        chip_to = target_chip(step, chip, core)
        p, j = work_of(chip_to)
        same = chip_to == chip
        mine = j // 4 == core
        for half in range(2):
            il = jnp.where(mine, 2 * (j - 4 * core) + half, 0)
            v_count = v_count + send(
                mine, same & (core == half),
                v_ref.at[il], vr_ref.at[chip], v_send, v_recv,
                (2 * z + half, chip_to),
            )
        o_counts = [o0, o1, o2]
        for outside in range(2):
            if outside:
                shift = jnp.where(core == 0, -8, 8)
                to_z = jnp.where(core == 0, (z + 3) % 4, (z + 1) % 4)
                inside = False
            else:
                shift, to_z, inside = 0, z, True
            for kind in range(5):
                ml = j + shift + kind - 2 - 4 * core
                hit = (ml >= 0) & (ml < 4)
                ml = jnp.where(hit, ml, 0)
                if kind in (0, 4):
                    to_core = 0 if kind == 0 else 1
                    first = 112 if kind == 0 else 0
                    e_count = e_count + send(
                        hit, (same & (core == to_core)) if inside else (same & False),
                        o_ref.at[ml, pl.ds(first, E_ROWS)], er_ref.at[chip], e_send, e_recv,
                        (2 * to_z + to_core, chip_to),
                    )
                else:
                    first, rows = O_SPAN[kind - 1]
                    o_counts[kind - 1] = o_counts[kind - 1] + send(
                        hit, (same & (core == o_core)) if inside else (same & False),
                        o_ref.at[ml, pl.ds(first, rows)],
                        or_ref.at[kind - 1, chip, pl.ds(first, rows)],
                        o_send.at[kind - 1], o_recv.at[kind - 1],
                        (2 * to_z + o_core, chip_to),
                    )
        return (v_count, *o_counts, e_count)

    v_count, o0, o1, o2, e_count = lax.fori_loop(0, 16, send_rest, (0, 0, 0, 0, 0))

    pltpu.make_async_copy(tr_ref.at[1], tr_ref.at[1], t_recv).wait()
    rim = []
    for slot, device in ((2, down), (0, up)):
        copy = pltpu.make_async_remote_copy(
            src_ref=tr_ref.at[1], dst_ref=tr_ref.at[slot],
            send_sem=f_send.at[slot // 2], recv_sem=f_recv.at[slot // 2],
            device_id=device, device_id_type=MESH,
        )
        copy.start()
        rim.append(copy)

    forwards = []
    for kind in range(3):
        first, rows = O_SPAN[kind]
        part = or_ref.at[kind, pl.ds(8 * core, 8), pl.ds(first, rows)]
        pltpu.make_async_copy(part, part, o_recv.at[kind]).wait()
        copy = pltpu.make_async_remote_copy(
            src_ref=part, dst_ref=part,
            send_sem=h_send.at[kind], recv_sem=h_recv.at[kind],
            device_id=(2 * z + 1 - core, chip), device_id_type=MESH,
        )
        copy.start()
        forwards.append(copy)

    pltpu.make_async_copy(vr_ref, vr_ref, v_recv).wait()
    pltpu.make_async_copy(er_ref, er_ref, e_recv).wait()
    for kind, copy in enumerate(forwards):
        first, rows = O_SPAN[kind]
        part = or_ref.at[kind, pl.ds(8 * (1 - core), 8), pl.ds(first, rows)]
        pltpu.make_async_copy(part, part, h_recv.at[kind]).wait()
        copy.wait_send()
    for copy in rim:
        copy.wait_send()
    for slot in (0, 2):
        pltpu.make_async_copy(tr_ref.at[slot], tr_ref.at[slot], f_recv.at[slot // 2]).wait()
    drain(t_count, t_ref.at[0, 0], t_send)
    drain(v_count, v_ref.at[0], v_send)
    drain(e_count, o_ref.at[0, pl.ds(0, E_ROWS)], e_send)
    for kind, count in enumerate((o0, o1, o2)):
        drain(count, o_ref.at[0, pl.ds(0, O_SPAN[kind][1])], o_send.at[kind])


def gather(t_pack, v_pack, o_pack):
    bf = jnp.bfloat16
    dma = pltpu.SemaphoreType.DMA
    return pl.pallas_call(
        gather_kernel,
        out_shape=(
            jax.ShapeDtypeStruct((3, 16, T_ROWS, BLK), bf),
            jax.ShapeDtypeStruct((16, V_ROWS, BLK), bf),
            jax.ShapeDtypeStruct((3, 16, O_ROWS, BLK), bf),
            jax.ShapeDtypeStruct((16, E_ROWS, BLK), bf),
        ),
        in_specs=[pl.BlockSpec(memory_space=pl.ANY)] * 3,
        out_specs=[pl.BlockSpec(memory_space=pl.ANY)] * 4,
        scratch_shapes=[
            dma, dma, dma, dma, dma((3,)), dma((3,)), dma, dma,
            dma((2,)), dma((2,)), dma((3,)), dma((3,)),
        ],
        compiler_params=pltpu.CompilerParams(collective_id=0, has_side_effects=True),
        name="gather_blocks",
    )(t_pack, v_pack, o_pack)


def contract_kernel(core_ref, t_ref, v_ref, o_ref, e_ref, out_ref, tc, vv, col, w, prod):
    f32, bf = jnp.float32, jnp.bfloat16
    core = core_ref[0]

    def pair_up(low, high, row):
        both = jnp.concatenate([low[row : row + 24], high[row : row + 24]], axis=0)
        return both.astype(bf)

    def spread(q, carry):
        rows = pl.ds(pl.multiple_of(q * 48, 16), 48)
        for g in range(3):
            low = t_ref[g, 2 * q].astype(f32)
            high = t_ref[g, 2 * q + 1].astype(f32)
            for h in range(5):
                tc[g, rows, h * BLK : (h + 1) * BLK] = pair_up(low, high, h * 24)
        low, high = v_ref[2 * q].astype(f32), v_ref[2 * q + 1].astype(f32)
        for g in range(3):
            vv[g, rows, :] = pair_up(low, high, g * 24)
        for kind in range(3):
            low = o_ref[kind, 2 * q].astype(f32)
            high = o_ref[kind, 2 * q + 1].astype(f32)
            for k in range(2):
                for g in range(3):
                    column = 2 * kind + k + g - 1
                    if 0 <= column < 6:
                        at = pl.ds(pl.multiple_of((2 - g) * BLK + q * 48, 16), 48)
                        col[column, at, :] = pair_up(low, high, (3 * k + g) * 24)
        low, high = e_ref[2 * q].astype(f32), e_ref[2 * q + 1].astype(f32)

        @pl.when(core == 0)
        def _():
            col[0, rows, :] = pair_up(low, high, 8)

        @pl.when(core == 1)
        def _():
            col[5, pl.ds(pl.multiple_of(2 * BLK + q * 48, 16), 48), :] = pair_up(low, high, 0)

        return carry

    lax.fori_loop(0, 8, spread, 0)

    for o in range(7):
        total = None
        for g in range(3):
            h = o - g
            if 0 <= h < 5:
                term = jnp.dot(
                    vv[g], tc[g, :, h * BLK : (h + 1) * BLK], preferred_element_type=f32
                )
                total = term if total is None else total + term
        w[:, o * BLK : (o + 1) * BLK] = total.astype(bf)
    for h in range(5):
        prod[h] = jnp.dot(
            w[:, h * BLK : (h + 3) * BLK], col[core + h], preferred_element_type=f32
        )

    def regroup(b, carry):
        rows = pl.ds(pl.multiple_of(b * 24, 8), 24)
        parts = [prod[h, rows, :] for h in range(5)]
        parts.append(jnp.zeros((T_ROWS - 120, BLK), f32))
        out_ref[b] = jnp.concatenate(parts, axis=0).astype(bf)
        return carry

    lax.fori_loop(0, 16, regroup, 0)


def contract(core, t_all, v_all, o_all, e_all):
    bf = jnp.bfloat16
    vmem = pl.BlockSpec(memory_space=pltpu.VMEM)
    return pl.pallas_call(
        contract_kernel,
        out_shape=jax.ShapeDtypeStruct((16, T_ROWS, BLK), bf),
        in_specs=[pl.BlockSpec(memory_space=pltpu.SMEM)] + [vmem] * 4,
        out_specs=vmem,
        scratch_shapes=[
            pltpu.VMEM((3, BLK, 5 * BLK), bf),
            pltpu.VMEM((3, BLK, BLK), bf),
            pltpu.VMEM((6, 3 * BLK, BLK), bf),
            pltpu.VMEM((BLK, 7 * BLK), bf),
            pltpu.VMEM((5, BLK, BLK), jnp.float32),
        ],
        compiler_params=pltpu.CompilerParams(vmem_limit_bytes=VMEM_LIMIT),
        cost_estimate=pl.CostEstimate(
            flops=30 * 2 * BLK**3, bytes_accessed=14_000_000, transcendentals=0
        ),
        name="contract_blocks",
    )(core, t_all, v_all, o_all, e_all)


def scatter_kernel(y_ref, out_ref, send_sem, recv_sem):
    a, chip, z, core = place()
    p_me, j_me = work_of(chip)
    to_core = j_me // 4
    il_me = 2 * (j_me % 4) + core
    bar = pltpu.get_barrier_semaphore()
    plane_barrier(bar, a, z, chip)
    pl.semaphore_wait(bar, 31)

    def one(step, count):
        chip_to = target_chip(step, chip, core)
        return count + send(
            chip_to >= 0, (chip_to == chip) & (to_core == core),
            y_ref.at[chip_to], out_ref.at[p_me, il_me], send_sem, recv_sem,
            (2 * z + to_core, chip_to),
        )

    count = lax.fori_loop(0, 16, one, 0)
    pltpu.make_async_copy(out_ref, out_ref, recv_sem).wait()
    drain(count, y_ref.at[0], send_sem)


def scatter(y):
    return pl.pallas_call(
        scatter_kernel,
        out_shape=jax.ShapeDtypeStruct((2, 8, T_ROWS, BLK), jnp.bfloat16),
        in_specs=[pl.BlockSpec(memory_space=pl.ANY)],
        out_specs=pl.BlockSpec(memory_space=pl.ANY),
        scratch_shapes=[pltpu.SemaphoreType.DMA, pltpu.SemaphoreType.DMA],
        compiler_params=pltpu.CompilerParams(collective_id=1, has_side_effects=True),
        name="scatter_rows",
    )(y)


def local_kernel(y_ref, t_ref, out_ref):
    f32 = jnp.float32
    lane = lax.broadcasted_iota(jnp.int32, (8, 128), 1)
    top = lax.broadcasted_iota(jnp.int32, (8, 128), 0) == 0
    out = jnp.zeros((8, 128), f32)
    for p in range(2):
        for q in range(2):
            def add(i, acc):
                both = y_ref[p, i].astype(f32) * t_ref[q, i].astype(f32)
                return acc + jnp.sum(both.reshape(T_ROWS // 8, 8, BLK), axis=0)

            total = lax.fori_loop(0, 8, add, jnp.zeros((8, BLK), f32))
            out = out + jnp.where(top & (lane == 2 * p + q), jnp.sum(total), 0.0)
    out_ref[...] = out


def local_sums(y_rows, t_pack):
    vmem = pl.BlockSpec(memory_space=pltpu.VMEM)
    return pl.pallas_call(
        local_kernel,
        out_shape=jax.ShapeDtypeStruct((8, 128), jnp.float32),
        in_specs=[vmem, vmem],
        out_specs=vmem,
        compiler_params=pltpu.CompilerParams(vmem_limit_bytes=VMEM_LIMIT),
        name="local_sums",
    )(y_rows, t_pack)


def total_kernel(x_ref, out_ref, slots, held, slots2, send_sem, recv_sem, send_sem2, recv_sem2):
    a, chip, _, _ = place()
    bar = pltpu.get_barrier_semaphore()

    def hello_chip(k, carry):
        greet(bar, a, (chip + k) % 16)
        return carry

    lax.fori_loop(1, 16, hello_chip, 0)

    def hello_group(k, carry):
        greet(bar, (a + k) % 8, chip)
        return carry

    lax.fori_loop(1, 8, hello_group, 0)
    pl.semaphore_wait(bar, 22)

    slots[chip] = x_ref[...]

    def to_chip(k, carry):
        pltpu.make_async_remote_copy(
            src_ref=x_ref, dst_ref=slots.at[chip], send_sem=send_sem, recv_sem=recv_sem,
            device_id=(a, (chip + k) % 16), device_id_type=MESH,
        ).start()
        return carry

    lax.fori_loop(1, 16, to_chip, 0)
    part = slots.at[pl.ds(0, 15)]
    pltpu.make_async_copy(part, part, recv_sem).wait()
    total = slots[0]
    for k in range(1, 16):
        total = total + slots[k]
    held[...] = total
    slots2[a] = total

    def to_group(k, carry):
        pltpu.make_async_remote_copy(
            src_ref=held, dst_ref=slots2.at[a], send_sem=send_sem2, recv_sem=recv_sem2,
            device_id=((a + k) % 8, chip), device_id_type=MESH,
        ).start()
        return carry

    lax.fori_loop(1, 8, to_group, 0)
    part2 = slots2.at[pl.ds(0, 7)]
    pltpu.make_async_copy(part2, part2, recv_sem2).wait()
    total = slots2[0]
    for k in range(1, 8):
        total = total + slots2[k]
    out_ref[...] = total
    pltpu.make_async_copy(part, part, send_sem).wait()
    pltpu.make_async_copy(part2, part2, send_sem2).wait()


def total_sums(x):
    vmem = pl.BlockSpec(memory_space=pltpu.VMEM)
    dma = pltpu.SemaphoreType.DMA
    return pl.pallas_call(
        total_kernel,
        out_shape=jax.ShapeDtypeStruct((8, 128), jnp.float32),
        in_specs=[vmem],
        out_specs=vmem,
        scratch_shapes=[
            pltpu.VMEM((16, 8, 128), jnp.float32),
            pltpu.VMEM((8, 128), jnp.float32),
            pltpu.VMEM((8, 8, 128), jnp.float32),
            dma, dma, dma, dma,
        ],
        compiler_params=pltpu.CompilerParams(collective_id=2, has_side_effects=True),
        name="total_sums",
    )(x)


def shards(tensor, occupied, virtual, tensor_mask, occupied_mask, virtual_mask):
    bf = jnp.bfloat16
    a = lax.axis_index("ba")

    def pattern(mask):
        return lax.dynamic_slice_in_dim(mask, a * 8, 8, 0).astype(bf)[:, :, None, None]

    tensor_pattern = pattern(tensor_mask)
    masked = (tensor * tensor_pattern[None]).reshape(2, 8, 120, BLK)
    t_pack = jnp.pad(masked, ((0, 0), (0, 0), (0, T_ROWS - 120), (0, 0)))
    v_pack = jnp.pad(
        (virtual * pattern(virtual_mask)).reshape(8, 72, BLK), ((0, 0), (0, V_ROWS - 72), (0, 0))
    )
    o_pack = (occupied * pattern(occupied_mask)).reshape(4, O_ROWS, BLK)
    t_all, v_all, o_all, e_all = gather(t_pack, v_pack, o_pack)
    core = (a % 2).astype(jnp.int32).reshape(1)
    y = contract(core, t_all, v_all, o_all, e_all)
    y_rows = scatter(y)
    sums = total_sums(local_sums(y_rows, t_pack))
    product = y_rows[:, :, :120].reshape(2, 8, HB, 24, BLK) * tensor_pattern[None]
    coupling = sums[0, :4].reshape(2, 2) / math.sqrt(BASIS * HB * BLK)
    return (product, coupling)


def solution(mesh):
    placed = (
        P(None, "ba", None, "bb", None),
        P("ba", None, "bb", None),
        P("ba", None, "bb", None),
        P(),
        P(),
        P(),
    )
    return jax.shard_map(
        shards,
        mesh=mesh,
        in_specs=placed,
        out_specs=(P(None, "ba", None, "bb", None), P()),
        check_vma=False,
    )
```

```python
import math

import jax
import jax.numpy as jnp
from jax import lax
from jax.experimental import pallas as pl
from jax.experimental.pallas import tpu as pltpu
from jax.sharding import PartitionSpec as P

BASIS = 24576
BLK = 384
HB = 5
MESH = pl.DeviceIdType.MESH
VMEM_LIMIT = 56 * 1024 * 1024

ROWS = 24
T_ROWS = 128
V_ROWS = 80
O_ROWS = 144
E_ROWS = 32
O_SPAN = ((16, 128), (0, 144), (0, 128))

ORDER = (
    (0, 0), (2, 2), (1, 0), (0, 1), (3, 0), (0, 3), (1, 1), (3, 3),
    (1, 3), (3, 1), (2, 0), (0, 2), (2, 1), (1, 2), (2, 3), (3, 2),
)


def pick(table, index):
    value = 0
    for position, entry in enumerate(table):
        if entry:
            value = value + jnp.where(index == position, entry, 0)
    return value


def chip_of(p, j):
    x = jnp.where(j < 4, j, 7 - j)
    y = jnp.where(j < 4, p, 3 - p)
    return y * 4 + x


def work_of(chip):
    x, y = chip % 4, chip // 4
    upper = y >= 2
    j = jnp.where(upper, 7 - x, x)
    p = jnp.where(upper, 3 - y, y)
    return p, j


def target_chip(step, chip, core):
    dx, dy = pick([d[0] for d in ORDER], step), pick([d[1] for d in ORDER], step)
    ex = jnp.where(core == 0, dx, dy)
    ey = jnp.where(core == 0, dy, dx)
    return ((chip // 4 + ey) % 4) * 4 + (chip % 4 + ex) % 4


def place():
    a, chip = lax.axis_index("ba"), lax.axis_index("bb")
    return a, chip, a // 2, a % 2


def greet(bar, a, b):
    pl.semaphore_signal(bar, inc=1, device_id=(a, b), device_id_type=MESH)


def plane_barrier(bar, a, z, chip):
    def hello(k, carry):
        other_a, other_chip = 2 * z + k // 16, k % 16

        @pl.when(jnp.logical_not((other_a == a) & (other_chip == chip)))
        def _():
            greet(bar, other_a, other_chip)

        return carry

    lax.fori_loop(0, 32, hello, 0)


def drain(count, ref, sem):
    def one(k, carry):
        pltpu.make_async_copy(ref, ref, sem).wait()
        return carry

    lax.fori_loop(0, count, one, 0)


def send(cond, is_self, src, dst, send_sem, recv_sem, device):
    @pl.when(cond & is_self)
    def _():
        pltpu.make_async_copy(src, dst, recv_sem).start()

    @pl.when(cond & jnp.logical_not(is_self))
    def _():
        pltpu.make_async_remote_copy(
            src_ref=src, dst_ref=dst, send_sem=send_sem, recv_sem=recv_sem,
            device_id=device, device_id_type=MESH,
        ).start()

    return jnp.where(cond & jnp.logical_not(is_self), 1, 0)


def source_row(p, core):
    return jnp.where(p == 0, 3 * core, 1 + core)


def rpa_kernel(
    tm_ref, om_ref, vm_ref, t_ref, v_ref, o_ref, y_ref, c_ref,
    tr, vr, oc, er, t_loc, tc, vv, col, w, prod, y_send, slots, held, slots2,
    loc_sem, t_send, t_recv, v_send, v_recv, o_send, o_recv, e_send, e_recv,
    f_send, f_recv, h_send, h_recv, g_send, g_recv, i_send, i_recv,
    y_out, y_in, s_send, s_recv, s_send2, s_recv2,
):
    f32, bf = jnp.float32, jnp.bfloat16
    a, chip, z, core = place()
    p_me, j_me = work_of(chip)
    s_me = 16 * z + 2 * j_me + core
    bar = pltpu.get_barrier_semaphore()
    plane_barrier(bar, a, z, chip)

    def hello_group(k, carry):
        greet(bar, (2 * z + 2 + k) % 8, chip)
        return carry

    lax.fori_loop(0, 6, hello_group, 0)

    @pl.when(j_me < 2)
    def _():
        def hello(k, carry):
            greet(bar, (2 * z + 7) % 8, k)
            return carry

        lax.fori_loop(0, 16, hello, 0)

    @pl.when(j_me >= 6)
    def _():
        def hello(k, carry):
            greet(bar, (2 * z + 2) % 8, k)
            return carry

        lax.fori_loop(0, 16, hello, 0)

    t_copy = pltpu.make_async_copy(t_ref, t_loc, loc_sem)
    t_copy.start()

    up_z = jnp.where(s_me % 16 < 15, z, (z + 1) % 4)
    up_j = jnp.where(core == 0, j_me, (j_me + 1) % 8)
    down_z = jnp.where(s_me % 16 > 0, z, (z + 3) % 4)
    down_j = jnp.where(core == 1, j_me, (j_me + 7) % 8)
    up = (2 * up_z + 1 - core, chip_of(p_me, up_j))
    down = (2 * down_z + 1 - core, chip_of(p_me, down_j))
    twin = (2 * z + 1 - core, chip)
    partner = (a, chip_of(1 - p_me, j_me))

    pl.semaphore_wait(bar, 45)

    y_me = chip // 4
    p_want = jnp.where((y_me == 0) | (y_me == 3), 0, 1)
    core_want = jnp.where(y_me < 2, 0, 1)

    def planes(j):
        outer_z = jnp.where(core == 0, (z + 3) % 4, (z + 1) % 4)
        return ((j, z, True), (j + jnp.where(core == 0, -8, 8), outer_z, False))

    def send_occ(step, counts):
        counts = list(counts)
        chip_to = target_chip(step, chip, core)
        p, j = work_of(chip_to)
        for j_rel, to_z, inside in planes(j):
            for kind in range(3):
                first, rows = O_SPAN[kind]
                ml = j_rel + kind - 1 - 4 * core
                hit = (ml >= 0) & (ml < 4) & (p == p_want)
                ml = jnp.where(hit, ml, 0)
                own = (chip_to == chip) & (core == core_want)
                counts[kind] = counts[kind] + send(
                    hit, own if inside else (own & False),
                    o_ref.at[ml, pl.ds(first, rows)],
                    oc.at[kind, chip, pl.ds(first, rows)],
                    o_send.at[kind], o_recv.at[kind],
                    (2 * to_z + core_want, chip_to),
                )
        return tuple(counts)

    o_counts = lax.fori_loop(0, 16, send_occ, (0, 0, 0))

    def send_t(step, count):
        chip_to = target_chip(step, chip, core)
        p, j = work_of(chip_to)
        mine = j // 4 == core
        pair = jnp.where(mine, j - 4 * core, 0)
        for half in range(2):
            count = count + send(
                mine, (chip_to == chip) & (core == half),
                t_ref.at[p, pair, pl.ds(112 * half, T_ROWS)], tr.at[1, chip], t_send, t_recv,
                (2 * z + half, chip_to),
            )
        return count

    t_count = lax.fori_loop(0, 16, send_t, 0)

    def part(kind, row):
        first, rows = O_SPAN[kind]
        return oc.at[kind, pl.ds(4 * row, 4), pl.ds(first, rows)]

    def hand_on(kind, row, device, send_sem, recv_sem):
        copy = pltpu.make_async_remote_copy(
            src_ref=part(kind, row), dst_ref=part(kind, row),
            send_sem=send_sem.at[kind], recv_sem=recv_sem.at[kind],
            device_id=device, device_id_type=MESH,
        )
        copy.start()
        return copy

    def arrived(ref, sem):
        pltpu.make_async_copy(ref, ref, sem).wait()

    copies = []
    for kind in range(3):
        row = source_row(p_me, core)
        arrived(part(kind, row), o_recv.at[kind])
        copies.append(hand_on(kind, row, partner, g_send, g_recv))
        copies.append(hand_on(kind, row, twin, h_send, h_recv))

    arrived(tr.at[1], t_recv)
    for slot, device in ((2, down), (0, up)):
        copy = pltpu.make_async_remote_copy(
            src_ref=tr.at[1], dst_ref=tr.at[slot],
            send_sem=f_send.at[slot // 2], recv_sem=f_recv.at[slot // 2],
            device_id=device, device_id_type=MESH,
        )
        copy.start()
        copies.append(copy)

    def send_rest(step, counts):
        v_count, e_count = counts
        chip_to = target_chip(step, chip, core)
        p, j = work_of(chip_to)
        same = chip_to == chip
        mine = j // 4 == core
        pair = jnp.where(mine, j - 4 * core, 0)
        for half in range(2):
            v_count = v_count + send(
                mine, same & (core == half),
                v_ref.at[pair, pl.ds(64 * half, V_ROWS)], vr.at[chip], v_send, v_recv,
                (2 * z + half, chip_to),
            )
        for j_rel, to_z, inside in planes(j):
            for to_core, first, kind in ((0, 112, -2), (1, 0, 2)):
                ml = j_rel + kind - 4 * core
                hit = (ml >= 0) & (ml < 4)
                ml = jnp.where(hit, ml, 0)
                own = same & (core == to_core)
                e_count = e_count + send(
                    hit, own if inside else (own & False),
                    o_ref.at[ml, pl.ds(first, E_ROWS)], er.at[chip], e_send, e_recv,
                    (2 * to_z + to_core, chip_to),
                )
        return v_count, e_count

    v_count, e_count = lax.fori_loop(0, 16, send_rest, (0, 0))

    for kind in range(3):
        row = source_row(1 - p_me, core)
        arrived(part(kind, row), g_recv.at[kind])
        copies.append(hand_on(kind, row, twin, i_send, i_recv))

    def joined(low, high, row, factor):
        both = jnp.concatenate([low[row : row + ROWS], high[row : row + ROWS]], axis=0)
        return (both * factor).astype(bf)

    def window(q):
        return pl.ds(pl.multiple_of(q * 2 * ROWS, 16), 2 * ROWS)

    def flag(ref, block, entry):
        return ref[(block + 64) % 64, entry].astype(f32)

    def shifted(ref, odd, rows):
        full = ref.astype(f32)
        return jnp.where(odd, full[8 : 8 + rows], full[:rows])

    def spread_t(g):
        factors = [flag(tm_ref, s_me + g - 1, h) for h in range(HB)]
        odd = (core == 1) if g == 1 else (core == 0)

        def one(q, carry):
            low = shifted(tr[g, 2 * q], odd, 120)
            high = shifted(tr[g, 2 * q + 1], odd, 120)
            for h in range(HB):
                tc[g, window(q), h * BLK : (h + 1) * BLK] = joined(low, high, h * ROWS, factors[h])
            return carry

        lax.fori_loop(0, 8, one, 0)

    spread_t(1)

    arrived(vr, v_recv)
    v_factors = [flag(vm_ref, s_me, g) for g in range(3)]

    def spread_v(q, carry):
        low = shifted(vr[2 * q], core == 1, 72)
        high = shifted(vr[2 * q + 1], core == 1, 72)
        for g in range(3):
            vv[g, window(q), :] = joined(low, high, g * ROWS, v_factors[g])
        return carry

    lax.fori_loop(0, 8, spread_v, 0)

    arrived(er, e_recv)
    edge_block = jnp.where(core == 0, s_me - 3, s_me + 3)
    edge_factor = jnp.where(core == 0, flag(om_ref, edge_block, 2), flag(om_ref, edge_block, 0))

    def spread_e(q, carry):
        low, high = er[2 * q].astype(f32), er[2 * q + 1].astype(f32)

        @pl.when(core == 0)
        def _():
            col[0, window(q), :] = joined(low, high, 8, edge_factor)

        @pl.when(core == 1)
        def _():
            at = pl.ds(pl.multiple_of(2 * BLK + q * 2 * ROWS, 16), 2 * ROWS)
            col[5, at, :] = joined(low, high, 0, edge_factor)

        return carry

    lax.fori_loop(0, 8, spread_e, 0)

    for kind in range(3):
        arrived(part(kind, source_row(p_me, 1 - core)), h_recv.at[kind])
        arrived(part(kind, source_row(1 - p_me, 1 - core)), i_recv.at[kind])
        first, rows = O_SPAN[kind]
        wanted = [
            (k, g, 2 * kind + k + g - 1)
            for k in range(2) for g in range(3)
            if 0 <= 2 * kind + k + g - 1 < 6
        ]
        base = 16 * z + 2 * (j_me + kind - 1)
        factors = [flag(om_ref, base + k, g) for k, g, _ in wanted]

        def spread_o(q, carry):
            low = oc[kind, 2 * q, first : first + rows].astype(f32)
            high = oc[kind, 2 * q + 1, first : first + rows].astype(f32)
            for (k, g, column), factor in zip(wanted, factors):
                at = pl.ds(pl.multiple_of((2 - g) * BLK + q * 2 * ROWS, 16), 2 * ROWS)
                col[column, at, :] = joined(low, high, (3 * k + g) * ROWS - first, factor)
            return carry

        lax.fori_loop(0, 8, spread_o, 0)

    for slot in (0, 2):
        arrived(tr.at[slot], f_recv.at[slot // 2])
        spread_t(slot)

    for o in range(7):
        total = None
        for g in range(3):
            h = o - g
            if 0 <= h < HB:
                term = jnp.dot(
                    vv[g], tc[g, :, h * BLK : (h + 1) * BLK], preferred_element_type=f32
                )
                total = term if total is None else total + term
        w[:, o * BLK : (o + 1) * BLK] = total.astype(bf)
    for h in range(HB):
        block = jnp.dot(
            w[:, h * BLK : (h + 3) * BLK], col[core + h], preferred_element_type=f32
        )
        prod[h] = block * flag(tm_ref, s_me, h)

    to_core = j_me // 4
    il_me = 2 * (j_me % 4) + core

    def regroup(step, count):
        chip_to = target_chip(step, chip, core)
        rows = pl.ds(pl.multiple_of(chip_to * ROWS, 8), ROWS)
        pieces = [prod[h, rows, :] for h in range(HB)]
        pieces.append(jnp.zeros((T_ROWS - HB * ROWS, BLK), f32))
        y_send[chip_to] = jnp.concatenate(pieces, axis=0).astype(bf)
        return count + send(
            chip_to >= 0, (chip_to == chip) & (to_core == core),
            y_send.at[chip_to], y_ref.at[p_me, il_me], y_out, y_in,
            (2 * z + to_core, chip_to),
        )

    y_count = lax.fori_loop(0, 16, regroup, 0)

    for copy in copies:
        copy.wait_send()
    drain(t_count, t_ref.at[0, 0, pl.ds(0, T_ROWS)], t_send)
    drain(v_count, v_ref.at[0, pl.ds(0, V_ROWS)], v_send)
    drain(e_count, o_ref.at[0, pl.ds(0, E_ROWS)], e_send)
    for kind, count in enumerate(o_counts):
        drain(count, o_ref.at[0, pl.ds(0, O_SPAN[kind][1])], o_send.at[kind])
    t_copy.wait()

    arrived(y_ref, y_in)

    def couple(pair, sums):
        sums = list(sums)
        ts = [t_loc[q, pair].astype(f32) for q in range(2)]
        for p in range(2):
            for half in range(2):
                y = y_ref[p, 2 * pair + half].astype(f32)[: HB * ROWS]
                for q in range(2):
                    both = y * ts[q][half * HB * ROWS : (half + 1) * HB * ROWS]
                    both = jnp.sum(both.reshape(HB * ROWS // 8, 8, BLK), axis=0)
                    sums[2 * p + q] = sums[2 * p + q] + both
        return tuple(sums)

    sums = lax.fori_loop(0, 4, couple, (jnp.zeros((8, BLK), f32),) * 4)
    lane = lax.broadcasted_iota(jnp.int32, (8, 128), 1)
    mine = jnp.zeros((8, 128), f32)
    for k in range(4):
        part_sum = sums[k][:, :128] + sums[k][:, 128:256] + sums[k][:, 256:]
        column = jnp.sum(part_sum, axis=1, keepdims=True)
        mine = mine + jnp.where(lane == k, column, 0.0)
    held[0] = mine
    slots[chip] = mine

    def to_chip(k, carry):
        pltpu.make_async_remote_copy(
            src_ref=held.at[0], dst_ref=slots.at[chip], send_sem=s_send, recv_sem=s_recv,
            device_id=(a, (chip + k) % 16), device_id_type=MESH,
        ).start()
        return carry

    lax.fori_loop(1, 16, to_chip, 0)
    most = slots.at[pl.ds(0, 15)]
    arrived(most, s_recv)
    total = slots[0]
    for k in range(1, 16):
        total = total + slots[k]
    held[1] = total
    slots2[a] = total

    def to_group(k, carry):
        pltpu.make_async_remote_copy(
            src_ref=held.at[1], dst_ref=slots2.at[a], send_sem=s_send2, recv_sem=s_recv2,
            device_id=((a + k) % 8, chip), device_id_type=MESH,
        ).start()
        return carry

    lax.fori_loop(1, 8, to_group, 0)
    most2 = slots2.at[pl.ds(0, 7)]
    arrived(most2, s_recv2)
    total = slots2[0]
    for k in range(1, 8):
        total = total + slots2[k]
    total = jnp.sum(total, axis=0, keepdims=True)
    c_ref[...] = jnp.broadcast_to(total, (8, 128)) / math.sqrt(BASIS * HB * BLK)
    arrived(most, s_send)
    arrived(most2, s_send2)
    drain(y_count, y_send.at[0], y_out)


def shards(tensor, occupied, virtual, tensor_mask, occupied_mask, virtual_mask):
    f32, bf = jnp.float32, jnp.bfloat16
    dma = pltpu.SemaphoreType.DMA
    vmem = pl.BlockSpec(memory_space=pltpu.VMEM)
    smem = pl.BlockSpec(memory_space=pltpu.SMEM)
    anywhere = pl.BlockSpec(memory_space=pl.ANY)
    product, coupling = pl.pallas_call(
        rpa_kernel,
        out_shape=(
            jax.ShapeDtypeStruct((2, 8, T_ROWS, BLK), bf),
            jax.ShapeDtypeStruct((8, 128), f32),
        ),
        in_specs=[smem] * 3 + [anywhere] * 3,
        out_specs=(vmem, vmem),
        scratch_shapes=[
            pltpu.VMEM((3, 16, T_ROWS, BLK), bf),
            pltpu.VMEM((16, V_ROWS, BLK), bf),
            pltpu.VMEM((3, 16, O_ROWS, BLK), bf),
            pltpu.VMEM((16, E_ROWS, BLK), bf),
            pltpu.VMEM((2, 4, 2 * HB * ROWS, BLK), bf),
            pltpu.VMEM((3, BLK, HB * BLK), bf),
            pltpu.VMEM((3, BLK, BLK), bf),
            pltpu.VMEM((6, 3 * BLK, BLK), bf),
            pltpu.VMEM((BLK, 7 * BLK), bf),
            pltpu.VMEM((HB, BLK, BLK), f32),
            pltpu.VMEM((16, T_ROWS, BLK), bf),
            pltpu.VMEM((16, 8, 128), f32),
            pltpu.VMEM((2, 8, 128), f32),
            pltpu.VMEM((8, 8, 128), f32),
            dma, dma, dma, dma, dma, dma((3,)), dma((3,)), dma, dma,
            dma((2,)), dma((2,)), dma((3,)), dma((3,)), dma((3,)), dma((3,)), dma((3,)), dma((3,)),
            dma, dma, dma, dma, dma, dma,
        ],
        compiler_params=pltpu.CompilerParams(
            collective_id=0, has_side_effects=True, vmem_limit_bytes=VMEM_LIMIT
        ),
        cost_estimate=pl.CostEstimate(
            flops=30 * 2 * BLK**3, bytes_accessed=20_000_000, transcendentals=0
        ),
        name="rpa_point",
    )(
        tensor_mask, occupied_mask, virtual_mask,
        tensor.reshape(2, 4, 2 * HB * ROWS, BLK),
        virtual.reshape(4, O_ROWS, BLK),
        occupied.reshape(4, O_ROWS, BLK),
    )
    rows = product[:, :, : HB * ROWS].reshape(2, 8, HB, ROWS, BLK)
    return (rows, coupling[0, :4].reshape(2, 2))


def solution(mesh):
    placed = (
        P(None, "ba", None, "bb", None),
        P("ba", None, "bb", None),
        P("ba", None, "bb", None),
        P(),
        P(),
        P(),
    )
    return jax.shard_map(
        shards,
        mesh=mesh,
        in_specs=placed,
        out_specs=(P(None, "ba", None, "bb", None), P()),
        check_vma=False,
    )
```

```python
import math

import jax
import jax.numpy as jnp
from jax import lax
from jax.experimental import pallas as pl
from jax.experimental.pallas import tpu as pltpu
from jax.sharding import PartitionSpec as P

BASIS = 24576
BLK = 384
HB = 5
MESH = pl.DeviceIdType.MESH
VMEM_LIMIT = 56 * 1024 * 1024

ROWS = 24
T_ROWS = 128
V_ROWS = 80
O_ROWS = 144
E_ROWS = 32
O_SPAN = ((16, 128), (0, 144), (0, 128))

ORDER = (
    (0, 0), (2, 2), (1, 0), (0, 1), (3, 0), (0, 3), (1, 1), (3, 3),
    (1, 3), (3, 1), (2, 0), (0, 2), (2, 1), (1, 2), (2, 3), (3, 2),
)


def pick(table, index):
    value = 0
    for position, entry in enumerate(table):
        if entry:
            value = value + jnp.where(index == position, entry, 0)
    return value


def chip_of(p, j):
    x = jnp.where(j < 4, j, 7 - j)
    y = jnp.where(j < 4, p, 3 - p)
    return y * 4 + x


def work_of(chip):
    x, y = chip % 4, chip // 4
    upper = y >= 2
    j = jnp.where(upper, 7 - x, x)
    p = jnp.where(upper, 3 - y, y)
    return p, j


def target_chip(step, chip, core):
    dx, dy = pick([d[0] for d in ORDER], step), pick([d[1] for d in ORDER], step)
    ex = jnp.where(core == 0, dx, dy)
    ey = jnp.where(core == 0, dy, dx)
    return ((chip // 4 + ey) % 4) * 4 + (chip % 4 + ex) % 4


def place():
    a, chip = lax.axis_index("ba"), lax.axis_index("bb")
    return a, chip, a // 2, a % 2


def greet(bar, a, b):
    pl.semaphore_signal(bar, inc=1, device_id=(a, b), device_id_type=MESH)


def plane_barrier(bar, a, core, chip):
    for k in range(16):
        greet(bar, a + 1 - 2 * core, k)

        @pl.when(chip != k)
        def _():
            greet(bar, a, k)


def drain(count, ref, sem):
    def one(k, carry):
        pltpu.make_async_copy(ref, ref, sem).wait()
        return carry

    lax.fori_loop(0, count, one, 0)


def send(cond, is_self, src, dst, send_sem, recv_sem, device):
    @pl.when(cond & is_self)
    def _():
        pltpu.make_async_copy(src, dst, recv_sem).start()

    @pl.when(cond & jnp.logical_not(is_self))
    def _():
        pltpu.make_async_remote_copy(
            src_ref=src, dst_ref=dst, send_sem=send_sem, recv_sem=recv_sem,
            device_id=device, device_id_type=MESH,
        ).start()

    return jnp.where(cond & jnp.logical_not(is_self), 1, 0)


def source_row(p, core):
    return jnp.where(p == 0, 3 * core, 1 + core)


def rpa_kernel(
    tm_ref, om_ref, vm_ref, t_ref, v_ref, o_ref, out_ref, c_ref,
    y_ref, tr, vr, oc, er, t_loc, tc, vv, col, w, prod, y_send, slots, held, slots2,
    loc_sem, t_send, t_recv, v_send, v_recv, o_send, o_recv, e_send, e_recv,
    f_send, f_recv, h_send, h_recv, g_send, g_recv, i_send, i_recv,
    y_out, y_in, s_send, s_recv, s_send2, s_recv2,
):
    f32, bf = jnp.float32, jnp.bfloat16
    a, chip, z, core = place()
    p_me, j_me = work_of(chip)
    s_me = 16 * z + 2 * j_me + core
    bar = pltpu.get_barrier_semaphore()
    plane_barrier(bar, a, core, chip)

    z_up, z_down = (z + 1) % 4, (z + 3) % 4
    for other_z in (z_up, z_down, (z + 2) % 4):
        greet(bar, 2 * other_z, chip)
        greet(bar, 2 * other_z + 1, chip)

    @pl.when(j_me < 2)
    def _():
        for k in range(16):
            greet(bar, 2 * z_down + 1, k)

    @pl.when(j_me >= 6)
    def _():
        for k in range(16):
            greet(bar, 2 * z_up, k)

    t_copy = pltpu.make_async_copy(t_ref, t_loc, loc_sem)
    t_copy.start()

    up_z = jnp.where(s_me % 16 < 15, z, (z + 1) % 4)
    up_j = jnp.where(core == 0, j_me, (j_me + 1) % 8)
    down_z = jnp.where(s_me % 16 > 0, z, (z + 3) % 4)
    down_j = jnp.where(core == 1, j_me, (j_me + 7) % 8)
    up = (2 * up_z + 1 - core, chip_of(p_me, up_j))
    down = (2 * down_z + 1 - core, chip_of(p_me, down_j))
    twin = (2 * z + 1 - core, chip)
    partner = (a, chip_of(1 - p_me, j_me))

    pl.semaphore_wait(bar, 45)

    y_me = chip // 4
    p_want = jnp.where((y_me == 0) | (y_me == 3), 0, 1)
    core_want = jnp.where(y_me < 2, 0, 1)

    def planes(j):
        outer_z = jnp.where(core == 0, (z + 3) % 4, (z + 1) % 4)
        return ((j, z, True), (j + jnp.where(core == 0, -8, 8), outer_z, False))

    def send_occ(step, counts):
        counts = list(counts)
        chip_to = target_chip(step, chip, core)
        p, j = work_of(chip_to)
        for j_rel, to_z, inside in planes(j):
            for kind in range(3):
                first, rows = O_SPAN[kind]
                ml = j_rel + kind - 1 - 4 * core
                hit = (ml >= 0) & (ml < 4) & (p == p_want)
                ml = jnp.where(hit, ml, 0)
                own = (chip_to == chip) & (core == core_want)
                counts[kind] = counts[kind] + send(
                    hit, own if inside else (own & False),
                    o_ref.at[ml, pl.ds(first, rows)],
                    oc.at[kind, chip, pl.ds(first, rows)],
                    o_send.at[kind], o_recv.at[kind, chip % 4],
                    (2 * to_z + core_want, chip_to),
                )
        return tuple(counts)

    o_counts = lax.fori_loop(0, 16, send_occ, (0, 0, 0))

    def send_t(step, count):
        chip_to = target_chip(step, chip, core)
        p, j = work_of(chip_to)
        mine = j // 4 == core
        pair = jnp.where(mine, j - 4 * core, 0)
        for half in range(2):
            count = count + send(
                mine, (chip_to == chip) & (core == half),
                t_ref.at[p, pair, pl.ds(112 * half, T_ROWS)], tr.at[1, chip], t_send, t_recv.at[chip // 4],
                (2 * z + half, chip_to),
            )
        return count

    t_count = lax.fori_loop(0, 16, send_t, 0)

    def part(kind, start, count=4):
        first, rows = O_SPAN[kind]
        return oc.at[kind, pl.ds(start, count), pl.ds(first, rows)]

    def hand_on(ref, device, send_sem, recv_sem):
        copy = pltpu.make_async_remote_copy(
            src_ref=ref, dst_ref=ref, send_sem=send_sem, recv_sem=recv_sem,
            device_id=device, device_id_type=MESH,
        )
        copy.start()
        return copy

    def arrived(ref, sem):
        pltpu.make_async_copy(ref, ref, sem).wait()

    def send_rest(step, counts):
        v_count, e_count = counts
        chip_to = target_chip(step, chip, core)
        p, j = work_of(chip_to)
        same = chip_to == chip
        mine = j // 4 == core
        pair = jnp.where(mine, j - 4 * core, 0)
        for half in range(2):
            v_count = v_count + send(
                mine, same & (core == half),
                v_ref.at[pair, pl.ds(64 * half, V_ROWS)], vr.at[chip], v_send, v_recv,
                (2 * z + half, chip_to),
            )
        for j_rel, to_z, inside in planes(j):
            for to_core, first, kind in ((0, 112, -2), (1, 0, 2)):
                ml = j_rel + kind - 4 * core
                hit = (ml >= 0) & (ml < 4)
                ml = jnp.where(hit, ml, 0)
                own = same & (core == to_core)
                e_count = e_count + send(
                    hit, own if inside else (own & False),
                    o_ref.at[ml, pl.ds(first, E_ROWS)], er.at[chip], e_send, e_recv,
                    (2 * to_z + to_core, chip_to),
                )
        return v_count, e_count

    v_count, e_count = lax.fori_loop(0, 16, send_rest, (0, 0))

    copies = []
    row_mine = 4 * source_row(p_me, core)
    row_partner = 4 * source_row(1 - p_me, core)
    for kind in range(3):
        for step in (0, 1, 3, 2):
            column = (chip + step) % 4
            ref = part(kind, row_mine + column, 1)
            arrived(ref, o_recv.at[kind, column])
            copies.append(hand_on(ref, partner, g_send.at[kind], g_recv.at[kind]))
        ref = part(kind, row_mine)
        copies.append(hand_on(ref, twin, h_send.at[kind], h_recv.at[kind]))

    for step in (0, 1, 3, 2):
        row = (chip // 4 + step) % 4
        group = pl.ds(4 * row, 4)
        arrived(tr.at[1, group], t_recv.at[row])
        for slot, device in ((2, down), (0, up)):
            copy = pltpu.make_async_remote_copy(
                src_ref=tr.at[1, group], dst_ref=tr.at[slot, group],
                send_sem=f_send.at[slot // 2], recv_sem=f_recv.at[slot // 2],
                device_id=device, device_id_type=MESH,
            )
            copy.start()
            copies.append(copy)

    def joined(low, high, row, factor):
        both = jnp.concatenate([low[row : row + ROWS], high[row : row + ROWS]], axis=0)
        return (both * factor).astype(bf)

    def window(q):
        return pl.ds(pl.multiple_of(q * 2 * ROWS, 16), 2 * ROWS)

    def flag(ref, block, entry):
        return ref[entry, (block + 64) % 64].astype(f32)

    def shifted(ref, odd, rows):
        full = ref.astype(f32)
        return jnp.where(odd, full[8 : 8 + rows], full[:rows])

    def spread_t(g):
        factors = [flag(tm_ref, s_me + g - 1, h) for h in range(HB)]
        odd = (core == 1) if g == 1 else (core == 0)

        def one(q, carry):
            low = shifted(tr[g, 2 * q], odd, 120)
            high = shifted(tr[g, 2 * q + 1], odd, 120)
            for h in range(HB):
                tc[g, window(q), h * BLK : (h + 1) * BLK] = joined(low, high, h * ROWS, factors[h])
            return carry

        lax.fori_loop(0, 8, one, 0)

    spread_t(1)

    for kind in range(3):
        ref = part(kind, row_partner)
        arrived(ref, g_recv.at[kind])
        copies.append(hand_on(ref, twin, i_send.at[kind], i_recv.at[kind]))

    arrived(vr, v_recv)
    v_factors = [flag(vm_ref, s_me, g) for g in range(3)]

    def spread_v(q, carry):
        low = shifted(vr[2 * q], core == 1, 72)
        high = shifted(vr[2 * q + 1], core == 1, 72)
        for g in range(3):
            vv[g, window(q), :] = joined(low, high, g * ROWS, v_factors[g])
        return carry

    lax.fori_loop(0, 8, spread_v, 0)

    for slot in (0, 2):
        arrived(tr.at[slot], f_recv.at[slot // 2])
        spread_t(slot)

    for o in range(7):
        total = None
        for g in range(3):
            h = o - g
            if 0 <= h < HB:
                term = jnp.dot(
                    vv[g], tc[g, :, h * BLK : (h + 1) * BLK], preferred_element_type=f32
                )
                total = term if total is None else total + term
        w[:, o * BLK : (o + 1) * BLK] = total.astype(bf)
    arrived(er, e_recv)
    edge_block = jnp.where(core == 0, s_me - 3, s_me + 3)
    edge_factor = jnp.where(core == 0, flag(om_ref, edge_block, 2), flag(om_ref, edge_block, 0))

    def spread_e(q, carry):
        low, high = er[2 * q].astype(f32), er[2 * q + 1].astype(f32)

        @pl.when(core == 0)
        def _():
            col[0, window(q), :] = joined(low, high, 8, edge_factor)

        @pl.when(core == 1)
        def _():
            at = pl.ds(pl.multiple_of(2 * BLK + q * 2 * ROWS, 16), 2 * ROWS)
            col[5, at, :] = joined(low, high, 0, edge_factor)

        return carry

    lax.fori_loop(0, 8, spread_e, 0)

    for kind in range(3):
        arrived(part(kind, 4 * source_row(p_me, 1 - core)), h_recv.at[kind])
        arrived(part(kind, 4 * source_row(1 - p_me, 1 - core)), i_recv.at[kind])
        first, rows = O_SPAN[kind]
        wanted = [
            (k, g, 2 * kind + k + g - 1)
            for k in range(2) for g in range(3)
            if 0 <= 2 * kind + k + g - 1 < 6
        ]
        base = 16 * z + 2 * (j_me + kind - 1)
        factors = [flag(om_ref, base + k, g) for k, g, _ in wanted]

        def spread_o(q, carry):
            low = oc[kind, 2 * q, first : first + rows].astype(f32)
            high = oc[kind, 2 * q + 1, first : first + rows].astype(f32)
            for (k, g, column), factor in zip(wanted, factors):
                at = pl.ds(pl.multiple_of((2 - g) * BLK + q * 2 * ROWS, 16), 2 * ROWS)
                col[column, at, :] = joined(low, high, (3 * k + g) * ROWS - first, factor)
            return carry

        lax.fori_loop(0, 8, spread_o, 0)

    for h in range(HB):
        block = jnp.dot(
            w[:, h * BLK : (h + 3) * BLK], col[core + h], preferred_element_type=f32
        )
        prod[h] = block * flag(tm_ref, s_me, h)

    to_core = j_me // 4
    il_me = 2 * (j_me % 4) + core

    def regroup(step, count):
        chip_to = target_chip(step, chip, core)
        rows = pl.ds(pl.multiple_of(chip_to * ROWS, 8), ROWS)
        pieces = [prod[h, rows, :] for h in range(HB)]
        pieces.append(jnp.zeros((T_ROWS - HB * ROWS, BLK), f32))
        y_send[chip_to] = jnp.concatenate(pieces, axis=0).astype(bf)
        return count + send(
            chip_to >= 0, (chip_to == chip) & (to_core == core),
            y_send.at[chip_to], y_ref.at[p_me, il_me], y_out, y_in,
            (2 * z + to_core, chip_to),
        )

    y_count = lax.fori_loop(0, 16, regroup, 0)

    for copy in copies:
        copy.wait_send()
    drain(t_count, t_ref.at[0, 0, pl.ds(0, T_ROWS)], t_send)
    drain(v_count, v_ref.at[0, pl.ds(0, V_ROWS)], v_send)
    drain(e_count, o_ref.at[0, pl.ds(0, E_ROWS)], e_send)
    for kind, count in enumerate(o_counts):
        drain(count, o_ref.at[0, pl.ds(0, O_SPAN[kind][1])], o_send.at[kind])
    t_copy.wait()

    arrived(y_ref, y_in)

    def couple(pair, sums):
        sums = list(sums)
        ts = [t_loc[q, pair].astype(f32) for q in range(2)]
        for p in range(2):
            for half in range(2):
                y = y_ref[p, 2 * pair + half][: HB * ROWS]
                out_ref[p, 2 * pair + half] = y
                y = y.astype(f32)
                for q in range(2):
                    both = y * ts[q][half * HB * ROWS : (half + 1) * HB * ROWS]
                    both = jnp.sum(both.reshape(HB * ROWS // 8, 8, BLK), axis=0)
                    sums[2 * p + q] = sums[2 * p + q] + both
        return tuple(sums)

    sums = lax.fori_loop(0, 4, couple, (jnp.zeros((8, BLK), f32),) * 4)
    row = lax.broadcasted_iota(jnp.int32, (8, 128), 0)
    lane = lax.broadcasted_iota(jnp.int32, (8, 128), 1)
    mine = jnp.zeros((8, 128), f32)
    for k in range(4):
        part_sum = sums[k][:, :128] + sums[k][:, 128:256] + sums[k][:, 256:]
        part_sum = jnp.sum(jnp.sum(part_sum, axis=0, keepdims=True), axis=1, keepdims=True)
        mine = mine + jnp.where((row == k // 2) & (lane == k % 2), part_sum, 0.0)
    held[0] = mine
    slots[chip] = mine

    def to_chip(k, carry):
        pltpu.make_async_remote_copy(
            src_ref=held.at[0], dst_ref=slots.at[chip], send_sem=s_send, recv_sem=s_recv,
            device_id=(a, (chip + k) % 16), device_id_type=MESH,
        ).start()
        return carry

    lax.fori_loop(1, 16, to_chip, 0)
    most = slots.at[pl.ds(0, 15)]
    arrived(most, s_recv)
    total = slots[0]
    for k in range(1, 16):
        total = total + slots[k]
    held[1] = total
    slots2[a] = total

    def to_group(k, carry):
        pltpu.make_async_remote_copy(
            src_ref=held.at[1], dst_ref=slots2.at[a], send_sem=s_send2, recv_sem=s_recv2,
            device_id=((a + k) % 8, chip), device_id_type=MESH,
        ).start()
        return carry

    lax.fori_loop(1, 8, to_group, 0)
    most2 = slots2.at[pl.ds(0, 7)]
    arrived(most2, s_recv2)
    total = slots2[0]
    for k in range(1, 8):
        total = total + slots2[k]
    c_ref[...] = total[:2, :2] / math.sqrt(BASIS * HB * BLK)
    arrived(most, s_send)
    arrived(most2, s_send2)
    drain(y_count, y_send.at[0], y_out)


def shards(tensor, occupied, virtual, tensor_mask, occupied_mask, virtual_mask):
    f32, bf = jnp.float32, jnp.bfloat16
    dma = pltpu.SemaphoreType.DMA
    vmem = pl.BlockSpec(memory_space=pltpu.VMEM)
    smem = pl.BlockSpec(memory_space=pltpu.SMEM)
    anywhere = pl.BlockSpec(memory_space=pl.ANY)
    product, coupling = pl.pallas_call(
        rpa_kernel,
        out_shape=(
            jax.ShapeDtypeStruct((2, 8, HB * ROWS, BLK), bf),
            jax.ShapeDtypeStruct((2, 2), f32),
        ),
        in_specs=[smem] * 3 + [anywhere] * 3,
        out_specs=(vmem, vmem),
        scratch_shapes=[
            pltpu.VMEM((2, 8, T_ROWS, BLK), bf),
            pltpu.VMEM((3, 16, T_ROWS, BLK), bf),
            pltpu.VMEM((16, V_ROWS, BLK), bf),
            pltpu.VMEM((3, 16, O_ROWS, BLK), bf),
            pltpu.VMEM((16, E_ROWS, BLK), bf),
            pltpu.VMEM((2, 4, 2 * HB * ROWS, BLK), bf),
            pltpu.VMEM((3, BLK, HB * BLK), bf),
            pltpu.VMEM((3, BLK, BLK), bf),
            pltpu.VMEM((6, 3 * BLK, BLK), bf),
            pltpu.VMEM((BLK, 7 * BLK), bf),
            pltpu.VMEM((HB, BLK, BLK), f32),
            pltpu.VMEM((16, T_ROWS, BLK), bf),
            pltpu.VMEM((16, 8, 128), f32),
            pltpu.VMEM((2, 8, 128), f32),
            pltpu.VMEM((8, 8, 128), f32),
            dma, dma, dma((4,)), dma, dma, dma((3,)), dma((3, 4)), dma, dma,
            dma((2,)), dma((2,)), dma((3,)), dma((3,)), dma((3,)), dma((3,)), dma((3,)), dma((3,)),
            dma, dma, dma, dma, dma, dma,
        ],
        compiler_params=pltpu.CompilerParams(
            collective_id=0, has_side_effects=True, vmem_limit_bytes=VMEM_LIMIT
        ),
        cost_estimate=pl.CostEstimate(
            flops=30 * 2 * BLK**3, bytes_accessed=20_000_000, transcendentals=0
        ),
        name="rpa_point",
    )(
        tensor_mask.T, occupied_mask.T, virtual_mask.T,
        tensor.reshape(2, 4, 2 * HB * ROWS, BLK),
        virtual.reshape(4, O_ROWS, BLK),
        occupied.reshape(4, O_ROWS, BLK),
    )
    return (product.reshape(2, 8, HB, ROWS, BLK), coupling)


def solution(mesh):
    placed = (
        P(None, "ba", None, "bb", None),
        P("ba", None, "bb", None),
        P("ba", None, "bb", None),
        P(),
        P(),
        P(),
    )
    return jax.shard_map(
        shards,
        mesh=mesh,
        in_specs=placed,
        out_specs=(P(None, "ba", None, "bb", None), P()),
        check_vma=False,
    )
```

```python
import math

import jax
import jax.numpy as jnp
from jax import lax
from jax.experimental import pallas as pl
from jax.experimental.pallas import tpu as pltpu
from jax.sharding import PartitionSpec as P

BASIS = 24576
BLK = 384
HB = 5
MESH = pl.DeviceIdType.MESH
VMEM_LIMIT = 56 * 1024 * 1024

ROWS = 24
T_ROWS = 128
V_ROWS = 80
O_ROWS = 144
E_ROWS = 32
O_SPAN = ((16, 128), (0, 144), (0, 128))

ORDER = (
    (0, 0), (2, 2), (1, 0), (0, 1), (3, 0), (0, 3), (1, 1), (3, 3),
    (1, 3), (3, 1), (2, 0), (0, 2), (2, 1), (1, 2), (2, 3), (3, 2),
)


def pick(table, index):
    value = 0
    for position, entry in enumerate(table):
        if entry:
            value = value + jnp.where(index == position, entry, 0)
    return value


def chip_of(p, j):
    x = jnp.where(j < 4, j, 7 - j)
    y = jnp.where(j < 4, p, 3 - p)
    return y * 4 + x


def work_of(chip):
    x, y = chip % 4, chip // 4
    upper = y >= 2
    j = jnp.where(upper, 7 - x, x)
    p = jnp.where(upper, 3 - y, y)
    return p, j


def target_chip(step, chip, core):
    dx, dy = pick([d[0] for d in ORDER], step), pick([d[1] for d in ORDER], step)
    ex = jnp.where(core == 0, dx, dy)
    ey = jnp.where(core == 0, dy, dx)
    return ((chip // 4 + ey) % 4) * 4 + (chip % 4 + ex) % 4


def place():
    a, chip = lax.axis_index("ba"), lax.axis_index("bb")
    return a, chip, a // 2, a % 2


def greet(bar, a, b):
    pl.semaphore_signal(bar, inc=1, device_id=(a, b), device_id_type=MESH)


def plane_barrier(bar, a, core, chip):
    for k in range(16):
        greet(bar, a + 1 - 2 * core, k)

        @pl.when(chip != k)
        def _():
            greet(bar, a, k)


def drain(count, ref, sem):
    def one(k, carry):
        pltpu.make_async_copy(ref, ref, sem).wait()
        return carry

    lax.fori_loop(0, count, one, 0)


def send(cond, is_self, src, dst, send_sem, recv_sem, device):
    @pl.when(cond & is_self)
    def _():
        pltpu.make_async_copy(src, dst, recv_sem).start()

    @pl.when(cond & jnp.logical_not(is_self))
    def _():
        pltpu.make_async_remote_copy(
            src_ref=src, dst_ref=dst, send_sem=send_sem, recv_sem=recv_sem,
            device_id=device, device_id_type=MESH,
        ).start()

    return jnp.where(cond & jnp.logical_not(is_self), 1, 0)


def source_row(p, core):
    return jnp.where(p == 0, 3 * core, 1 + core)


def rpa_kernel(
    tm_ref, om_ref, vm_ref, t_ref, v_ref, o_ref, out_ref, c_ref,
    y_ref, tr, vr, oc, er, t_loc, tc, vv, col, acc, w, prod, y_send, slots, held, slots2,
    loc_sem, t_send, t_recv, v_send, v_recv, o_send, o_recv, e_send, e_recv,
    f_send, f_recv, h_send, h_recv, g_send, g_recv, i_send, i_recv,
    y_out, y_in, s_send, s_recv, s_send2, s_recv2, k_send, k_recv,
):
    f32, bf = jnp.float32, jnp.bfloat16
    a, chip, z, core = place()
    p_me, j_me = work_of(chip)
    s_me = 16 * z + 2 * j_me + core
    bar = pltpu.get_barrier_semaphore()
    plane_barrier(bar, a, core, chip)

    z_up, z_down = (z + 1) % 4, (z + 3) % 4
    for other_z in (z_up, z_down, (z + 2) % 4):
        greet(bar, 2 * other_z, chip)
        greet(bar, 2 * other_z + 1, chip)

    @pl.when(j_me < 2)
    def _():
        for k in range(16):
            greet(bar, 2 * z_down + 1, k)

    @pl.when(j_me >= 6)
    def _():
        for k in range(16):
            greet(bar, 2 * z_up, k)

    t_copy = pltpu.make_async_copy(t_ref, t_loc, loc_sem)
    t_copy.start()

    up_z = jnp.where(s_me % 16 < 15, z, (z + 1) % 4)
    up_j = jnp.where(core == 0, j_me, (j_me + 1) % 8)
    down_z = jnp.where(s_me % 16 > 0, z, (z + 3) % 4)
    down_j = jnp.where(core == 1, j_me, (j_me + 7) % 8)
    up = (2 * up_z + 1 - core, chip_of(p_me, up_j))
    down = (2 * down_z + 1 - core, chip_of(p_me, down_j))
    twin = (2 * z + 1 - core, chip)
    partner = (a, chip_of(1 - p_me, j_me))

    pl.semaphore_wait(bar, 45)

    y_me = chip // 4
    p_want = jnp.where((y_me == 0) | (y_me == 3), 0, 1)
    core_want = jnp.where(y_me < 2, 0, 1)

    def planes(j):
        outer_z = jnp.where(core == 0, (z + 3) % 4, (z + 1) % 4)
        return ((j, z, True), (j + jnp.where(core == 0, -8, 8), outer_z, False))

    def send_occ(step, counts):
        counts = list(counts)
        chip_to = target_chip(step, chip, core)
        p, j = work_of(chip_to)
        for j_rel, to_z, inside in planes(j):
            for kind in range(3):
                first, rows = O_SPAN[kind]
                ml = j_rel + kind - 1 - 4 * core
                hit = (ml >= 0) & (ml < 4) & (p == p_want)
                ml = jnp.where(hit, ml, 0)
                own = (chip_to == chip) & (core == core_want)
                counts[kind] = counts[kind] + send(
                    hit, own if inside else (own & False),
                    o_ref.at[ml, pl.ds(first, rows)],
                    oc.at[kind, chip, pl.ds(first, rows)],
                    o_send.at[kind], o_recv.at[kind, chip % 4],
                    (2 * to_z + core_want, chip_to),
                )
        return tuple(counts)

    def send_t(step, count):
        chip_to = target_chip(step, chip, core)
        p, j = work_of(chip_to)
        mine = j // 4 == core
        pair = jnp.where(mine, j - 4 * core, 0)
        for half in range(2):
            count = count + send(
                mine, (chip_to == chip) & (core == half),
                t_ref.at[p, pair, pl.ds(112 * half, T_ROWS)], tr.at[1, chip], t_send, t_recv.at[chip // 4],
                (2 * z + half, chip_to),
            )
        return count

    def part(kind, start, count=4):
        first, rows = O_SPAN[kind]
        return oc.at[kind, pl.ds(start, count), pl.ds(first, rows)]

    def hand_on(ref, device, send_sem, recv_sem):
        copy = pltpu.make_async_remote_copy(
            src_ref=ref, dst_ref=ref, send_sem=send_sem, recv_sem=recv_sem,
            device_id=device, device_id_type=MESH,
        )
        copy.start()
        return copy

    def arrived(ref, sem):
        pltpu.make_async_copy(ref, ref, sem).wait()

    def send_v(step, counts):
        v_count = counts
        chip_to = target_chip(step, chip, core)
        p, j = work_of(chip_to)
        same = chip_to == chip
        mine = j // 4 == core
        pair = jnp.where(mine, j - 4 * core, 0)
        for half in range(2):
            v_count = v_count + send(
                mine & (p == p_want), same & (core == half),
                v_ref.at[pair, pl.ds(64 * half, V_ROWS)], vr.at[chip],
                v_send, v_recv.at[chip // 4],
                (2 * z + half, chip_to),
            )
        return v_count

    def send_e(step, counts):
        e_count = counts
        chip_to = target_chip(step, chip, core)
        p, j = work_of(chip_to)
        same = chip_to == chip
        for j_rel, to_z, inside in planes(j):
            for to_core, first, kind in ((0, 112, -2), (1, 0, 2)):
                ml = j_rel + kind - 4 * core
                hit = (ml >= 0) & (ml < 4) & (p == p_want)
                ml = jnp.where(hit, ml, 0)
                own = same & (core == to_core)
                e_count = e_count + send(
                    hit, own if inside else (own & False),
                    o_ref.at[ml, pl.ds(first, E_ROWS)], er.at[chip],
                    e_send, e_recv.at[chip // 4],
                    (2 * to_z + to_core, chip_to),
                )
        return e_count

    def pair_of_rows(p):
        return jnp.where(p == 0, 0, 1), jnp.where(p == 0, 3, 2)

    copies = []
    row_mine = 4 * source_row(p_me, core)
    row_partner = 4 * source_row(1 - p_me, core)
    t_count = lax.fori_loop(0, 16, send_t, 0)
    o_counts = lax.fori_loop(0, 16, send_occ, (0, 0, 0))
    v_count = lax.fori_loop(0, 16, send_v, 0)
    e_count = lax.fori_loop(0, 16, send_e, 0)
    for kind in range(3):
        for step in (0, 1, 3, 2):
            column = (chip + step) % 4
            ref = part(kind, row_mine + column, 1)
            arrived(ref, o_recv.at[kind, column])
            copies.append(hand_on(ref, partner, g_send.at[kind], g_recv.at[kind]))
        ref = part(kind, row_mine)
        copies.append(hand_on(ref, twin, h_send.at[kind], h_recv.at[kind]))

    for step in (0, 1, 3, 2):
        row = (chip // 4 + step) % 4
        group = pl.ds(4 * row, 4)
        arrived(tr.at[1, group], t_recv.at[row])
        for slot, device in ((2, down), (0, up)):
            copy = pltpu.make_async_remote_copy(
                src_ref=tr.at[1, group], dst_ref=tr.at[slot, group],
                send_sem=f_send.at[slot // 2], recv_sem=f_recv.at[slot // 2],
                device_id=device, device_id_type=MESH,
            )
            copy.start()
            copies.append(copy)

    for ref, rows_in, send_sem, recv_sem in (
        (vr, v_recv, k_send.at[0], k_recv.at[0]),
    ):
        for row in pair_of_rows(p_me):
            group = ref.at[pl.ds(4 * row, 4)]
            arrived(group, rows_in.at[row])
            copies.append(hand_on(group, partner, send_sem, recv_sem))

    for ref, rows_in, send_sem, recv_sem in (
        (er, e_recv, k_send.at[1], k_recv.at[1]),
    ):
        for row in pair_of_rows(p_me):
            group = ref.at[pl.ds(4 * row, 4)]
            arrived(group, rows_in.at[row])
            copies.append(hand_on(group, partner, send_sem, recv_sem))

    def joined(low, high, row, factor):
        both = jnp.concatenate([low[row : row + ROWS], high[row : row + ROWS]], axis=0)
        return (both * factor).astype(bf)

    def window(q):
        return pl.ds(pl.multiple_of(q * 2 * ROWS, 16), 2 * ROWS)

    def flag(ref, block, entry):
        return ref[entry, (block + 64) % 64].astype(f32)

    def shifted(ref, odd, rows):
        full = ref.astype(f32)
        return jnp.where(odd, full[8 : 8 + rows], full[:rows])

    def spread_t(g):
        factors = [flag(tm_ref, s_me + g - 1, h) for h in range(HB)]
        odd = (core == 1) if g == 1 else (core == 0)

        def one(q, carry):
            low = shifted(tr[g, 2 * q], odd, 120)
            high = shifted(tr[g, 2 * q + 1], odd, 120)
            for h in range(HB):
                tc[g, window(q), h * BLK : (h + 1) * BLK] = joined(low, high, h * ROWS, factors[h])
            return carry

        lax.fori_loop(0, 8, one, 0)

    spread_t(1)

    for kind in range(3):
        ref = part(kind, row_partner)
        arrived(ref, g_recv.at[kind])
        copies.append(hand_on(ref, twin, i_send.at[kind], i_recv.at[kind]))

    arrived(vr.at[pl.ds(0, 8)], k_recv.at[0])
    v_factors = [flag(vm_ref, s_me, g) for g in range(3)]

    def spread_v(q, carry):
        low = shifted(vr[2 * q], core == 1, 72)
        high = shifted(vr[2 * q + 1], core == 1, 72)
        for g in range(3):
            vv[g, window(q), :] = joined(low, high, g * ROWS, v_factors[g])
        return carry

    lax.fori_loop(0, 8, spread_v, 0)

    def term(g, o):
        h = o - g
        return jnp.dot(vv[g], tc[g, :, h * BLK : (h + 1) * BLK], preferred_element_type=f32)

    for o in range(1, 6):
        acc[o] = term(1, o)

    def neighbours(near, far):
        arrived(tr.at[near], f_recv.at[near // 2])
        spread_t(near)
        for o in range(near, near + HB):
            value = term(near, o)
            acc[o] = acc[o] + value if 1 <= o <= 5 else value
        arrived(tr.at[far], f_recv.at[far // 2])
        spread_t(far)
        for o in range(7):
            value = term(far, o) if far <= o < far + HB else None
            if 1 <= o <= 5 or near <= o < near + HB:
                value = acc[o] if value is None else acc[o] + value
            w[:, o * BLK : (o + 1) * BLK] = value.astype(bf)

    @pl.when(core == 0)
    def _():
        neighbours(2, 0)

    @pl.when(core == 1)
    def _():
        neighbours(0, 2)

    arrived(er.at[pl.ds(0, 8)], k_recv.at[1])
    edge_block = jnp.where(core == 0, s_me - 3, s_me + 3)
    edge_factor = jnp.where(core == 0, flag(om_ref, edge_block, 2), flag(om_ref, edge_block, 0))

    def spread_e(q, carry):
        low, high = er[2 * q].astype(f32), er[2 * q + 1].astype(f32)

        @pl.when(core == 0)
        def _():
            col[0, window(q), :] = joined(low, high, 8, edge_factor)

        @pl.when(core == 1)
        def _():
            at = pl.ds(pl.multiple_of(2 * BLK + q * 2 * ROWS, 16), 2 * ROWS)
            col[5, at, :] = joined(low, high, 0, edge_factor)

        return carry

    lax.fori_loop(0, 8, spread_e, 0)

    def spread_kind(kind):
        arrived(part(kind, 4 * source_row(p_me, 1 - core)), h_recv.at[kind])
        arrived(part(kind, 4 * source_row(1 - p_me, 1 - core)), i_recv.at[kind])
        first, rows = O_SPAN[kind]
        wanted = [
            (k, g, 2 * kind + k + g - 1)
            for k in range(2) for g in range(3)
            if 0 <= 2 * kind + k + g - 1 < 6
        ]
        base = 16 * z + 2 * (j_me + kind - 1)
        factors = [flag(om_ref, base + k, g) for k, g, _ in wanted]

        def spread_o(q, carry):
            low = oc[kind, 2 * q, first : first + rows].astype(f32)
            high = oc[kind, 2 * q + 1, first : first + rows].astype(f32)
            for (k, g, column), factor in zip(wanted, factors):
                at = pl.ds(pl.multiple_of((2 - g) * BLK + q * 2 * ROWS, 16), 2 * ROWS)
                col[column, at, :] = joined(low, high, (3 * k + g) * ROWS - first, factor)
            return carry

        lax.fori_loop(0, 8, spread_o, 0)

    to_core = j_me // 4
    il_me = 2 * (j_me % 4) + core

    def finish(blocks, first, rows, index):
        for h in blocks:
            block = jnp.dot(
                w[:, h * BLK : (h + 3) * BLK], col[core + h], preferred_element_type=f32
            )
            prod[h] = block * flag(tm_ref, s_me, h)

        def regroup(step, count):
            chip_to = target_chip(step, chip, core)
            at = pl.ds(pl.multiple_of(chip_to * ROWS, 8), ROWS)
            pieces = [prod[h, at, :] for h in blocks]
            if rows > len(blocks) * ROWS:
                pieces.append(jnp.zeros((rows - len(blocks) * ROWS, BLK), f32))
            window_to = pl.ds(first, rows)
            y_send[chip_to, window_to] = jnp.concatenate(pieces, axis=0).astype(bf)
            return count + send(
                chip_to >= 0, (chip_to == chip) & (to_core == core),
                y_send.at[chip_to, window_to], y_ref.at[p_me, il_me, window_to],
                y_out.at[index], y_in.at[index], (2 * z + to_core, chip_to),
            )

        return lax.fori_loop(0, 16, regroup, 0)

    spread_kind(0)
    spread_kind(1)
    y_count = finish((0, 1), 0, 48, 0)
    spread_kind(2)
    finish((2, 3, 4), 48, 80, 1)

    for copy in copies:
        copy.wait_send()
    drain(t_count, t_ref.at[0, 0, pl.ds(0, T_ROWS)], t_send)
    drain(v_count, v_ref.at[0, pl.ds(0, V_ROWS)], v_send)
    drain(e_count, o_ref.at[0, pl.ds(0, E_ROWS)], e_send)
    for kind, count in enumerate(o_counts):
        drain(count, o_ref.at[0, pl.ds(0, O_SPAN[kind][1])], o_send.at[kind])
    t_copy.wait()

    for index, (first, rows) in enumerate(((0, 48), (48, 80))):
        arrived(y_ref.at[:, :, pl.ds(first, rows)], y_in.at[index])

    def couple(pair, sums):
        sums = list(sums)
        ts = [t_loc[q, pair].astype(f32) for q in range(2)]
        for p in range(2):
            for half in range(2):
                y = y_ref[p, 2 * pair + half][: HB * ROWS]
                out_ref[p, 2 * pair + half] = y
                y = y.astype(f32)
                for q in range(2):
                    both = y * ts[q][half * HB * ROWS : (half + 1) * HB * ROWS]
                    both = jnp.sum(both.reshape(HB * ROWS // 8, 8, BLK), axis=0)
                    sums[2 * p + q] = sums[2 * p + q] + both
        return tuple(sums)

    sums = lax.fori_loop(0, 4, couple, (jnp.zeros((8, BLK), f32),) * 4)
    row = lax.broadcasted_iota(jnp.int32, (8, 128), 0)
    lane = lax.broadcasted_iota(jnp.int32, (8, 128), 1)
    mine = jnp.zeros((8, 128), f32)
    for k in range(4):
        part_sum = sums[k][:, :128] + sums[k][:, 128:256] + sums[k][:, 256:]
        part_sum = jnp.sum(jnp.sum(part_sum, axis=0, keepdims=True), axis=1, keepdims=True)
        mine = mine + jnp.where((row == k // 2) & (lane == k % 2), part_sum, 0.0)
    held[0] = mine
    slots[chip] = mine

    def to_chip(k, carry):
        pltpu.make_async_remote_copy(
            src_ref=held.at[0], dst_ref=slots.at[chip], send_sem=s_send, recv_sem=s_recv,
            device_id=(a, (chip + k) % 16), device_id_type=MESH,
        ).start()
        return carry

    lax.fori_loop(1, 16, to_chip, 0)
    most = slots.at[pl.ds(0, 15)]
    arrived(most, s_recv)
    total = slots[0]
    for k in range(1, 16):
        total = total + slots[k]
    held[1] = total
    slots2[a] = total

    def to_group(k, carry):
        pltpu.make_async_remote_copy(
            src_ref=held.at[1], dst_ref=slots2.at[a], send_sem=s_send2, recv_sem=s_recv2,
            device_id=((a + k) % 8, chip), device_id_type=MESH,
        ).start()
        return carry

    lax.fori_loop(1, 8, to_group, 0)
    most2 = slots2.at[pl.ds(0, 7)]
    arrived(most2, s_recv2)
    total = slots2[0]
    for k in range(1, 8):
        total = total + slots2[k]
    c_ref[...] = total[:2, :2] / math.sqrt(BASIS * HB * BLK)
    arrived(most, s_send)
    arrived(most2, s_send2)
    drain(y_count, y_send.at[0, pl.ds(0, 48)], y_out.at[0])
    drain(y_count, y_send.at[0, pl.ds(48, 80)], y_out.at[1])


def shards(tensor, occupied, virtual, tensor_mask, occupied_mask, virtual_mask):
    f32, bf = jnp.float32, jnp.bfloat16
    dma = pltpu.SemaphoreType.DMA
    vmem = pl.BlockSpec(memory_space=pltpu.VMEM)
    smem = pl.BlockSpec(memory_space=pltpu.SMEM)
    anywhere = pl.BlockSpec(memory_space=pl.ANY)
    product, coupling = pl.pallas_call(
        rpa_kernel,
        out_shape=(
            jax.ShapeDtypeStruct((2, 8, HB * ROWS, BLK), bf),
            jax.ShapeDtypeStruct((2, 2), f32),
        ),
        in_specs=[smem] * 3 + [anywhere] * 3,
        out_specs=(vmem, vmem),
        scratch_shapes=[
            pltpu.VMEM((2, 8, T_ROWS, BLK), bf),
            pltpu.VMEM((3, 16, T_ROWS, BLK), bf),
            pltpu.VMEM((16, V_ROWS, BLK), bf),
            pltpu.VMEM((3, 16, O_ROWS, BLK), bf),
            pltpu.VMEM((16, E_ROWS, BLK), bf),
            pltpu.VMEM((2, 4, 2 * HB * ROWS, BLK), bf),
            pltpu.VMEM((3, BLK, HB * BLK), bf),
            pltpu.VMEM((3, BLK, BLK), bf),
            pltpu.VMEM((6, 3 * BLK, BLK), bf),
            pltpu.VMEM((7, BLK, BLK), f32),
            pltpu.VMEM((BLK, 7 * BLK), bf),
            pltpu.VMEM((HB, BLK, BLK), f32),
            pltpu.VMEM((16, T_ROWS, BLK), bf),
            pltpu.VMEM((16, 8, 128), f32),
            pltpu.VMEM((2, 8, 128), f32),
            pltpu.VMEM((8, 8, 128), f32),
            dma, dma, dma((4,)), dma, dma((4,)), dma((3,)), dma((3, 4)), dma, dma((4,)),
            dma((2,)), dma((2,)), dma((3,)), dma((3,)), dma((3,)), dma((3,)), dma((3,)), dma((3,)),
            dma((2,)), dma((2,)), dma, dma, dma, dma, dma((2,)), dma((2,)),
        ],
        compiler_params=pltpu.CompilerParams(
            collective_id=0, has_side_effects=True, vmem_limit_bytes=VMEM_LIMIT
        ),
        cost_estimate=pl.CostEstimate(
            flops=30 * 2 * BLK**3, bytes_accessed=20_000_000, transcendentals=0
        ),
        name="rpa_point",
    )(
        tensor_mask.T, occupied_mask.T, virtual_mask.T,
        tensor.reshape(2, 4, 2 * HB * ROWS, BLK),
        virtual.reshape(4, O_ROWS, BLK),
        occupied.reshape(4, O_ROWS, BLK),
    )
    return (product.reshape(2, 8, HB, ROWS, BLK), coupling)


def solution(mesh):
    placed = (
        P(None, "ba", None, "bb", None),
        P("ba", None, "bb", None),
        P("ba", None, "bb", None),
        P(),
        P(),
        P(),
    )
    return jax.shard_map(
        shards,
        mesh=mesh,
        in_specs=placed,
        out_specs=(P(None, "ba", None, "bb", None), P()),
        check_vma=False,
    )
```

```python
import math

import jax
import jax.numpy as jnp
from jax import lax
from jax.experimental import pallas as pl
from jax.experimental.pallas import tpu as pltpu
from jax.sharding import PartitionSpec as P

BASIS = 24576
BLK = 384
HB = 5
MESH = pl.DeviceIdType.MESH
VMEM_LIMIT = 56 * 1024 * 1024

ROWS = 24
T_ROWS = 128
V_ROWS = 80
O_ROWS = 144
E_ROWS = 32
O_SPAN = ((16, 128), (0, 144), (0, 128))

T_ORDER = (
    (0, 0), (2, 2), (0, 1), (1, 0), (0, 3), (3, 0), (1, 1), (3, 2),
    (3, 1), (1, 3), (0, 2), (2, 0), (1, 2), (2, 1), (3, 3), (2, 3),
)
O_ORDER = (
    (0, 0), (2, 2), (1, 0), (0, 1), (3, 0), (0, 3), (1, 1), (3, 3),
    (1, 3), (3, 1), (2, 0), (0, 2), (2, 1), (1, 2), (2, 3), (3, 2),
)
V_ORDER = (
    (0, 0), (2, 2), (1, 0), (0, 1), (3, 0), (0, 3), (1, 1), (3, 3),
    (1, 3), (3, 1), (2, 0), (0, 2), (2, 1), (1, 2), (2, 3), (3, 2),
)
Y_ORDER = (
    (0, 0), (2, 2), (3, 0), (0, 3), (1, 0), (0, 1), (3, 3), (1, 1),
    (3, 1), (1, 3), (2, 0), (0, 2), (2, 3), (3, 2), (2, 1), (1, 2),
)


def pick(table, index):
    value = 0
    for position, entry in enumerate(table):
        if entry:
            value = value + jnp.where(index == position, entry, 0)
    return value


def chip_of(p, j):
    x = jnp.where(j < 4, j, 7 - j)
    y = jnp.where(j < 4, p, 3 - p)
    return y * 4 + x


def work_of(chip):
    x, y = chip % 4, chip // 4
    upper = y >= 2
    j = jnp.where(upper, 7 - x, x)
    p = jnp.where(upper, 3 - y, y)
    return p, j


def target_chip(order, step, chip, core):
    dx, dy = pick([d[0] for d in order], step), pick([d[1] for d in order], step)
    ex = jnp.where(core == 0, dx, dy)
    ey = jnp.where(core == 0, dy, dx)
    return ((chip // 4 + ey) % 4) * 4 + (chip % 4 + ex) % 4


def place():
    a, chip = lax.axis_index("ba"), lax.axis_index("bb")
    return a, chip, a // 2, a % 2


def greet(bar, a, b):
    pl.semaphore_signal(bar, inc=1, device_id=(a, b), device_id_type=MESH)


def plane_barrier(bar, a, core, chip):
    for k in range(16):
        greet(bar, a + 1 - 2 * core, k)

        @pl.when(chip != k)
        def _():
            greet(bar, a, k)


def drain(count, ref, sem):
    def one(k, carry):
        pltpu.make_async_copy(ref, ref, sem).wait()
        return carry

    lax.fori_loop(0, count, one, 0)


def send(cond, is_self, src, dst, send_sem, recv_sem, device):
    @pl.when(cond & is_self)
    def _():
        pltpu.make_async_copy(src, dst, recv_sem).start()

    @pl.when(cond & jnp.logical_not(is_self))
    def _():
        pltpu.make_async_remote_copy(
            src_ref=src, dst_ref=dst, send_sem=send_sem, recv_sem=recv_sem,
            device_id=device, device_id_type=MESH,
        ).start()

    return jnp.where(cond & jnp.logical_not(is_self), 1, 0)


def source_row(p, core):
    return jnp.where(p == 0, 3 * core, 1 + core)


def rpa_kernel(
    tm_ref, om_ref, vm_ref, t_ref, v_ref, o_ref, out_ref, c_ref,
    y_ref, tr, vr, oc, er, t_loc, tc, vv, col, acc, w, prod, y_send, slots, held, slots2,
    loc_sem, t_send, t_recv, v_send, v_recv, o_send, o_recv, e_send, e_recv,
    f_send, f_recv, h_send, h_recv, g_send, g_recv, i_send, i_recv,
    y_out, y_in, s_send, s_recv, s_send2, s_recv2, k_send, k_recv,
):
    f32, bf = jnp.float32, jnp.bfloat16
    a, chip, z, core = place()
    p_me, j_me = work_of(chip)
    s_me = 16 * z + 2 * j_me + core
    bar = pltpu.get_barrier_semaphore()
    plane_barrier(bar, a, core, chip)

    z_up, z_down = (z + 1) % 4, (z + 3) % 4
    for other_z in (z_up, z_down, (z + 2) % 4):
        greet(bar, 2 * other_z, chip)
        greet(bar, 2 * other_z + 1, chip)

    @pl.when(j_me < 2)
    def _():
        for k in range(16):
            greet(bar, 2 * z_down + 1, k)

    @pl.when(j_me >= 6)
    def _():
        for k in range(16):
            greet(bar, 2 * z_up, k)

    t_copy = pltpu.make_async_copy(t_ref, t_loc, loc_sem)
    t_copy.start()

    up_z = jnp.where(s_me % 16 < 15, z, (z + 1) % 4)
    up_j = jnp.where(core == 0, j_me, (j_me + 1) % 8)
    down_z = jnp.where(s_me % 16 > 0, z, (z + 3) % 4)
    down_j = jnp.where(core == 1, j_me, (j_me + 7) % 8)
    up = (2 * up_z + 1 - core, chip_of(p_me, up_j))
    down = (2 * down_z + 1 - core, chip_of(p_me, down_j))
    twin = (2 * z + 1 - core, chip)
    partner = (a, chip_of(1 - p_me, j_me))

    pl.semaphore_wait(bar, 45)

    y_me = chip // 4
    p_want = jnp.where((y_me == 0) | (y_me == 3), 0, 1)
    core_want = jnp.where(y_me < 2, 0, 1)

    def planes(j):
        outer_z = jnp.where(core == 0, (z + 3) % 4, (z + 1) % 4)
        return ((j, z, True), (j + jnp.where(core == 0, -8, 8), outer_z, False))

    def send_occ(kind):
        first, rows = O_SPAN[kind]

        def one(step, count):
            chip_to = target_chip(O_ORDER, step, chip, core)
            p, j = work_of(chip_to)
            own = (chip_to == chip) & (core == core_want)
            for j_rel, to_z, inside in planes(j):
                ml = j_rel + kind - 1 - 4 * core
                hit = (ml >= 0) & (ml < 4) & (p == p_want)
                ml = jnp.where(hit, ml, 0)
                count = count + send(
                    hit, own if inside else (own & False),
                    o_ref.at[ml, pl.ds(first, rows)],
                    oc.at[kind, chip, pl.ds(first, rows)],
                    o_send.at[kind], o_recv.at[kind, chip % 4],
                    (2 * to_z + core_want, chip_to),
                )
            return count

        return lax.fori_loop(0, 16, one, 0)

    def send_t(step, count):
        chip_to = target_chip(T_ORDER, step, chip, core)
        p, j = work_of(chip_to)
        mine = j // 4 == core
        pair = jnp.where(mine, j - 4 * core, 0)
        for half in range(2):
            count = count + send(
                mine, (chip_to == chip) & (core == half),
                t_ref.at[p, pair, pl.ds(112 * half, T_ROWS)], tr.at[1, chip], t_send, t_recv.at[chip // 4],
                (2 * z + half, chip_to),
            )
        return count

    def part(kind, start, count=4):
        first, rows = O_SPAN[kind]
        return oc.at[kind, pl.ds(start, count), pl.ds(first, rows)]

    def hand_on(ref, device, send_sem, recv_sem):
        copy = pltpu.make_async_remote_copy(
            src_ref=ref, dst_ref=ref, send_sem=send_sem, recv_sem=recv_sem,
            device_id=device, device_id_type=MESH,
        )
        copy.start()
        return copy

    def arrived(ref, sem):
        pltpu.make_async_copy(ref, ref, sem).wait()

    def send_v(step, counts):
        v_count = counts
        chip_to = target_chip(V_ORDER, step, chip, core)
        p, j = work_of(chip_to)
        same = chip_to == chip
        mine = j // 4 == core
        pair = jnp.where(mine, j - 4 * core, 0)
        for half in range(2):
            v_count = v_count + send(
                mine & (p == p_want), same & (core == half),
                v_ref.at[pair, pl.ds(64 * half, V_ROWS)], vr.at[chip],
                v_send, v_recv.at[chip // 4],
                (2 * z + half, chip_to),
            )
        return v_count

    def send_e(step, counts):
        e_count = counts
        chip_to = target_chip(V_ORDER, step, chip, core)
        p, j = work_of(chip_to)
        same = chip_to == chip
        for j_rel, to_z, inside in planes(j):
            for to_core, first, kind in ((0, 112, -2), (1, 0, 2)):
                ml = j_rel + kind - 4 * core
                hit = (ml >= 0) & (ml < 4) & (p == p_want)
                ml = jnp.where(hit, ml, 0)
                own = same & (core == to_core)
                e_count = e_count + send(
                    hit, own if inside else (own & False),
                    o_ref.at[ml, pl.ds(first, E_ROWS)], er.at[chip],
                    e_send, e_recv.at[chip // 4],
                    (2 * to_z + to_core, chip_to),
                )
        return e_count

    def pair_of_rows(p):
        return jnp.where(p == 0, 0, 1), jnp.where(p == 0, 3, 2)

    copies = []
    row_mine = 4 * source_row(p_me, core)
    row_partner = 4 * source_row(1 - p_me, core)
    t_count = lax.fori_loop(0, 16, send_t, 0)
    o_counts = [send_occ(kind) for kind in (0, 1)]
    v_count = lax.fori_loop(0, 16, send_v, 0)
    o_counts.append(send_occ(2))
    e_count = lax.fori_loop(0, 16, send_e, 0)
    for kind in range(3):
        for step in (0, 1, 3, 2):
            column = (chip + step) % 4
            ref = part(kind, row_mine + column, 1)
            arrived(ref, o_recv.at[kind, column])
            copies.append(hand_on(ref, partner, g_send.at[kind], g_recv.at[kind]))
        ref = part(kind, row_mine)
        copies.append(hand_on(ref, twin, h_send.at[kind], h_recv.at[kind]))

    for step in (0, 1, 3, 2):
        row = (chip // 4 + step) % 4
        group = pl.ds(4 * row, 4)
        arrived(tr.at[1, group], t_recv.at[row])
        for slot, device in ((2, down), (0, up)):
            copy = pltpu.make_async_remote_copy(
                src_ref=tr.at[1, group], dst_ref=tr.at[slot, group],
                send_sem=f_send.at[slot // 2], recv_sem=f_recv.at[slot // 2],
                device_id=device, device_id_type=MESH,
            )
            copy.start()
            copies.append(copy)

    for ref, rows_in, send_sem, recv_sem in (
        (vr, v_recv, k_send.at[0], k_recv.at[0]),
    ):
        for row in pair_of_rows(p_me):
            group = ref.at[pl.ds(4 * row, 4)]
            arrived(group, rows_in.at[row])
            copies.append(hand_on(group, partner, send_sem, recv_sem))

    for ref, rows_in, send_sem, recv_sem in (
        (er, e_recv, k_send.at[1], k_recv.at[1]),
    ):
        for row in pair_of_rows(p_me):
            group = ref.at[pl.ds(4 * row, 4)]
            arrived(group, rows_in.at[row])
            copies.append(hand_on(group, partner, send_sem, recv_sem))

    def joined(low, high, row, factor):
        both = jnp.concatenate([low[row : row + ROWS], high[row : row + ROWS]], axis=0)
        return (both * factor).astype(bf)

    def window(q):
        return pl.ds(pl.multiple_of(q * 2 * ROWS, 16), 2 * ROWS)

    def flag(ref, block, entry):
        return ref[entry, (block + 64) % 64].astype(f32)

    def shifted(ref, odd, rows):
        full = ref.astype(f32)
        return jnp.where(odd, full[8 : 8 + rows], full[:rows])

    def spread_t(g):
        factors = [flag(tm_ref, s_me + g - 1, h) for h in range(HB)]
        odd = (core == 1) if g == 1 else (core == 0)

        def one(q, carry):
            low = shifted(tr[g, 2 * q], odd, 120)
            high = shifted(tr[g, 2 * q + 1], odd, 120)
            for h in range(HB):
                tc[g, window(q), h * BLK : (h + 1) * BLK] = joined(low, high, h * ROWS, factors[h])
            return carry

        lax.fori_loop(0, 8, one, 0)

    spread_t(1)

    for kind in range(3):
        ref = part(kind, row_partner)
        arrived(ref, g_recv.at[kind])
        copies.append(hand_on(ref, twin, i_send.at[kind], i_recv.at[kind]))

    arrived(vr.at[pl.ds(0, 8)], k_recv.at[0])
    v_factors = [flag(vm_ref, s_me, g) for g in range(3)]

    def spread_v(q, carry):
        low = shifted(vr[2 * q], core == 1, 72)
        high = shifted(vr[2 * q + 1], core == 1, 72)
        for g in range(3):
            vv[g, window(q), :] = joined(low, high, g * ROWS, v_factors[g])
        return carry

    lax.fori_loop(0, 8, spread_v, 0)

    def term(g, o):
        h = o - g
        return jnp.dot(vv[g], tc[g, :, h * BLK : (h + 1) * BLK], preferred_element_type=f32)

    for o in range(1, 6):
        acc[o] = term(1, o)

    def neighbours(near, far):
        arrived(tr.at[near], f_recv.at[near // 2])
        spread_t(near)
        for o in range(near, near + HB):
            value = term(near, o)
            acc[o] = acc[o] + value if 1 <= o <= 5 else value
        arrived(tr.at[far], f_recv.at[far // 2])
        spread_t(far)
        for o in range(7):
            value = term(far, o) if far <= o < far + HB else None
            if 1 <= o <= 5 or near <= o < near + HB:
                value = acc[o] if value is None else acc[o] + value
            w[:, o * BLK : (o + 1) * BLK] = value.astype(bf)

    @pl.when(core == 0)
    def _():
        neighbours(2, 0)

    @pl.when(core == 1)
    def _():
        neighbours(0, 2)

    arrived(er.at[pl.ds(0, 8)], k_recv.at[1])
    edge_block = jnp.where(core == 0, s_me - 3, s_me + 3)
    edge_factor = jnp.where(core == 0, flag(om_ref, edge_block, 2), flag(om_ref, edge_block, 0))

    def spread_e(q, carry):
        low, high = er[2 * q].astype(f32), er[2 * q + 1].astype(f32)

        @pl.when(core == 0)
        def _():
            col[0, window(q), :] = joined(low, high, 8, edge_factor)

        @pl.when(core == 1)
        def _():
            at = pl.ds(pl.multiple_of(2 * BLK + q * 2 * ROWS, 16), 2 * ROWS)
            col[5, at, :] = joined(low, high, 0, edge_factor)

        return carry

    lax.fori_loop(0, 8, spread_e, 0)

    def spread_kind(kind):
        arrived(part(kind, 4 * source_row(p_me, 1 - core)), h_recv.at[kind])
        arrived(part(kind, 4 * source_row(1 - p_me, 1 - core)), i_recv.at[kind])
        first, rows = O_SPAN[kind]
        wanted = [
            (k, g, 2 * kind + k + g - 1)
            for k in range(2) for g in range(3)
            if 0 <= 2 * kind + k + g - 1 < 6
        ]
        base = 16 * z + 2 * (j_me + kind - 1)
        factors = [flag(om_ref, base + k, g) for k, g, _ in wanted]

        def spread_o(q, carry):
            low = oc[kind, 2 * q, first : first + rows].astype(f32)
            high = oc[kind, 2 * q + 1, first : first + rows].astype(f32)
            for (k, g, column), factor in zip(wanted, factors):
                at = pl.ds(pl.multiple_of((2 - g) * BLK + q * 2 * ROWS, 16), 2 * ROWS)
                col[column, at, :] = joined(low, high, (3 * k + g) * ROWS - first, factor)
            return carry

        lax.fori_loop(0, 8, spread_o, 0)

    to_core = j_me // 4
    il_me = 2 * (j_me % 4) + core

    def finish(blocks, first, rows, index):
        for h in blocks:
            block = jnp.dot(
                w[:, h * BLK : (h + 3) * BLK], col[core + h], preferred_element_type=f32
            )
            prod[h] = block * flag(tm_ref, s_me, h)

        def regroup(step, count):
            chip_to = target_chip(Y_ORDER, step, chip, core)
            at = pl.ds(pl.multiple_of(chip_to * ROWS, 8), ROWS)
            pieces = [prod[h, at, :] for h in blocks]
            if rows > len(blocks) * ROWS:
                pieces.append(jnp.zeros((rows - len(blocks) * ROWS, BLK), f32))
            window_to = pl.ds(first, rows)
            y_send[chip_to, window_to] = jnp.concatenate(pieces, axis=0).astype(bf)
            return count + send(
                chip_to >= 0, (chip_to == chip) & (to_core == core),
                y_send.at[chip_to, window_to], y_ref.at[p_me, il_me, window_to],
                y_out.at[index], y_in.at[index], (2 * z + to_core, chip_to),
            )

        return lax.fori_loop(0, 16, regroup, 0)

    spread_kind(0)
    spread_kind(1)
    y_count = finish((0, 1), 0, 48, 0)
    spread_kind(2)
    finish((2, 3, 4), 48, 80, 1)

    for copy in copies:
        copy.wait_send()
    drain(t_count, t_ref.at[0, 0, pl.ds(0, T_ROWS)], t_send)
    drain(v_count, v_ref.at[0, pl.ds(0, V_ROWS)], v_send)
    drain(e_count, o_ref.at[0, pl.ds(0, E_ROWS)], e_send)
    for kind, count in enumerate(o_counts):
        drain(count, o_ref.at[0, pl.ds(0, O_SPAN[kind][1])], o_send.at[kind])
    t_copy.wait()

    for index, (first, rows) in enumerate(((0, 48), (48, 80))):
        arrived(y_ref.at[:, :, pl.ds(first, rows)], y_in.at[index])

    def couple(pair, sums):
        sums = list(sums)
        ts = [t_loc[q, pair].astype(f32) for q in range(2)]
        for p in range(2):
            for half in range(2):
                y = y_ref[p, 2 * pair + half][: HB * ROWS]
                out_ref[p, 2 * pair + half] = y
                y = y.astype(f32)
                for q in range(2):
                    both = y * ts[q][half * HB * ROWS : (half + 1) * HB * ROWS]
                    both = jnp.sum(both.reshape(HB * ROWS // 8, 8, BLK), axis=0)
                    sums[2 * p + q] = sums[2 * p + q] + both
        return tuple(sums)

    sums = lax.fori_loop(0, 4, couple, (jnp.zeros((8, BLK), f32),) * 4)
    row = lax.broadcasted_iota(jnp.int32, (8, 128), 0)
    lane = lax.broadcasted_iota(jnp.int32, (8, 128), 1)
    mine = jnp.zeros((8, 128), f32)
    for k in range(4):
        part_sum = sums[k][:, :128] + sums[k][:, 128:256] + sums[k][:, 256:]
        part_sum = jnp.sum(jnp.sum(part_sum, axis=0, keepdims=True), axis=1, keepdims=True)
        mine = mine + jnp.where((row == k // 2) & (lane == k % 2), part_sum, 0.0)
    held[0] = mine
    slots[chip] = mine

    def to_chip(k, carry):
        pltpu.make_async_remote_copy(
            src_ref=held.at[0], dst_ref=slots.at[chip], send_sem=s_send, recv_sem=s_recv,
            device_id=(a, (chip + k) % 16), device_id_type=MESH,
        ).start()
        return carry

    lax.fori_loop(1, 16, to_chip, 0)
    most = slots.at[pl.ds(0, 15)]
    arrived(most, s_recv)
    total = slots[0]
    for k in range(1, 16):
        total = total + slots[k]
    held[1] = total
    slots2[a] = total

    def to_group(k, carry):
        pltpu.make_async_remote_copy(
            src_ref=held.at[1], dst_ref=slots2.at[a], send_sem=s_send2, recv_sem=s_recv2,
            device_id=((a + k) % 8, chip), device_id_type=MESH,
        ).start()
        return carry

    lax.fori_loop(1, 8, to_group, 0)
    most2 = slots2.at[pl.ds(0, 7)]
    arrived(most2, s_recv2)
    total = slots2[0]
    for k in range(1, 8):
        total = total + slots2[k]
    c_ref[...] = total[:2, :2] / math.sqrt(BASIS * HB * BLK)
    arrived(most, s_send)
    arrived(most2, s_send2)
    drain(y_count, y_send.at[0, pl.ds(0, 48)], y_out.at[0])
    drain(y_count, y_send.at[0, pl.ds(48, 80)], y_out.at[1])


def shards(tensor, occupied, virtual, tensor_mask, occupied_mask, virtual_mask):
    f32, bf = jnp.float32, jnp.bfloat16
    dma = pltpu.SemaphoreType.DMA
    vmem = pl.BlockSpec(memory_space=pltpu.VMEM)
    smem = pl.BlockSpec(memory_space=pltpu.SMEM)
    anywhere = pl.BlockSpec(memory_space=pl.ANY)
    product, coupling = pl.pallas_call(
        rpa_kernel,
        out_shape=(
            jax.ShapeDtypeStruct((2, 8, HB * ROWS, BLK), bf),
            jax.ShapeDtypeStruct((2, 2), f32),
        ),
        in_specs=[smem] * 3 + [anywhere] * 3,
        out_specs=(vmem, vmem),
        scratch_shapes=[
            pltpu.VMEM((2, 8, T_ROWS, BLK), bf),
            pltpu.VMEM((3, 16, T_ROWS, BLK), bf),
            pltpu.VMEM((16, V_ROWS, BLK), bf),
            pltpu.VMEM((3, 16, O_ROWS, BLK), bf),
            pltpu.VMEM((16, E_ROWS, BLK), bf),
            pltpu.VMEM((2, 4, 2 * HB * ROWS, BLK), bf),
            pltpu.VMEM((3, BLK, HB * BLK), bf),
            pltpu.VMEM((3, BLK, BLK), bf),
            pltpu.VMEM((6, 3 * BLK, BLK), bf),
            pltpu.VMEM((7, BLK, BLK), f32),
            pltpu.VMEM((BLK, 7 * BLK), bf),
            pltpu.VMEM((HB, BLK, BLK), f32),
            pltpu.VMEM((16, T_ROWS, BLK), bf),
            pltpu.VMEM((16, 8, 128), f32),
            pltpu.VMEM((2, 8, 128), f32),
            pltpu.VMEM((8, 8, 128), f32),
            dma, dma, dma((4,)), dma, dma((4,)), dma((3,)), dma((3, 4)), dma, dma((4,)),
            dma((2,)), dma((2,)), dma((3,)), dma((3,)), dma((3,)), dma((3,)), dma((3,)), dma((3,)),
            dma((2,)), dma((2,)), dma, dma, dma, dma, dma((2,)), dma((2,)),
        ],
        compiler_params=pltpu.CompilerParams(
            collective_id=0, has_side_effects=True, vmem_limit_bytes=VMEM_LIMIT
        ),
        cost_estimate=pl.CostEstimate(
            flops=30 * 2 * BLK**3, bytes_accessed=20_000_000, transcendentals=0
        ),
        name="rpa_point",
    )(
        tensor_mask.T, occupied_mask.T, virtual_mask.T,
        tensor.reshape(2, 4, 2 * HB * ROWS, BLK),
        virtual.reshape(4, O_ROWS, BLK),
        occupied.reshape(4, O_ROWS, BLK),
    )
    return (product.reshape(2, 8, HB, ROWS, BLK), coupling)


def solution(mesh):
    placed = (
        P(None, "ba", None, "bb", None),
        P("ba", None, "bb", None),
        P("ba", None, "bb", None),
        P(),
        P(),
        P(),
    )
    return jax.shard_map(
        shards,
        mesh=mesh,
        in_specs=placed,
        out_specs=(P(None, "ba", None, "bb", None), P()),
        check_vma=False,
    )
```
